256 devices in a mesh: level: 4 (over z_lo), seq: 16 (over y, z_hi, core), dp: 4 (over x).
Axes of the slice: x: 4, y: 4, z: 8 (z_hi: 2, z_lo: 4; z = z_hi * 4 + z_lo), core: 2. Of those that a mesh axis runs over, the one named last changes fastest.
Arguments:
- feats: bfloat16 [4, 512, 5120], P('dp'), may hold values from -6 to 6
- gen_gain: float32 [5120], replicated, may hold values from 0.25 to 1.75
- gen_weight: bfloat16 [5120, 64], replicated, may hold values from -0.078125 to 0.078125
- noise: float32 [4, 4, 512, 64], P('level', 'dp'), may hold values from -6 to 6
- sigmas: float32 [4], P('level'), may hold values from 0.1 to 10
- level_weights: float32 [4], P('level'), may hold values from 0.3 to 3
- embed: bfloat16 [2, 64, 5120], replicated, may hold values from -0.75 to 0.75
- proj_in: bfloat16 [2, 3, 5120, 4096], P(None, None, ('level', 'dp'), 'seq'), may hold values from -0.078125 to 0.078125
- proj_out: bfloat16 [2, 4096, 5120], P(None, 'seq', ('level', 'dp')), may hold values from -0.09375 to 0.09375
- head_out: bfloat16 [2, 5120, 64], replicated, may hold values from -0.078125 to 0.078125
- qk_gain: float32 [2, 2, 128], replicated, may hold values from 0.5 to 2.5
Outputs:
- grad_h: bfloat16 [4, 512, 5120], P('dp', 'seq')
- grad_weight: float32 [5120, 64], P('dp')
- grad_gain: float32 [5120], P('dp')
The draws below stay inside these ranges and needn't reach their ends.
All inputs are finite; a program needn't handle non-finite values.
Results may differ from the reference program's by a relative error of at most 0.019.
Values may be sent and summed in bfloat16 or wider, within the bound.
A program may use at most 192 MiB of HBM per device.

```python
import math
import jax
import jax.numpy as jnp
from jax import lax

D = 5120
C = 64
HD = 128
HEADS = 32
SLAB = 512
LEVELS = 4
SAMPLES = 4


def block_levels(key, dims, split, smallest, top_value):
    level = 1.0
    for position, blocks in split:
        heights = jax.random.uniform(jax.random.fold_in(jax.random.fold_in(key, 6), position), (blocks,), jnp.float32, smallest / len(split), top_value / len(split))
        level = level * jnp.repeat(jnp.exp(heights), dims[position] // blocks).reshape((-1,) + (1,) * (len(dims) - 1 - position))
    return level


def gaussian(rng, shape, deviation, most, cuts=(), dtype=jnp.bfloat16):
    level = block_levels(rng, shape, cuts, -0.22, 0.18) if cuts else 1.0
    entries = jax.random.normal(rng, shape, jnp.float32) * deviation * level
    return jnp.minimum(jnp.maximum(entries, -most), most).astype(dtype)


def setup_inputs(seed: int = 0) -> dict:
    splits = jax.random.split(jax.random.key(seed), 12)
    feats = gaussian(splits[0], (SAMPLES, SLAB, D), 1.0, 6.0, ((0, 4),))
    gen_gain = jnp.clip(1.0 + 0.15 * jax.random.normal(splits[1], (D,), jnp.float32), 0.25, 1.75)
    gen_weight = gaussian(splits[2], (D, C), D ** -0.5, 0.078125)
    noise = gaussian(splits[3], (LEVELS, SAMPLES, SLAB, C), 1.0, 6.0, ((0, 4), (1, 4)), jnp.float32)
    sigmas = jnp.clip(jnp.exp(math.log(10.0) - 4.6051702 * jax.random.uniform(splits[4], (LEVELS,), jnp.float32) ** block_levels(splits[4], (LEVELS,), ((0, 4),), -0.2, 0.2)), 0.1, 10.0)
    level_weights = jnp.clip(jnp.exp(math.log(3.0) - 2.3025851 * jax.random.uniform(splits[5], (LEVELS,), jnp.float32) ** block_levels(splits[5], (LEVELS,), ((0, 4),), -0.2, 0.2)), 0.3, 3.0)
    embed = gaussian(splits[6], (2, C, D), C ** -0.5, 0.75)
    proj_in = gaussian(splits[7], (2, 3, D, HEADS * HD), D ** -0.5, 0.078125, ((2, 16), (3, 16)))
    proj_out = gaussian(splits[8], (2, HEADS * HD, D), (HEADS * HD) ** -0.5, 0.09375, ((1, 16), (2, 16)))
    head_out = gaussian(splits[9], (2, D, C), D ** -0.5, 0.078125)
    qk_gain = jnp.clip(jax.random.uniform(splits[10], (2, 2, HD), jnp.float32, 0.5, 2.5), 0.5, 2.5)
    return dict(feats=feats, gen_gain=gen_gain, gen_weight=gen_weight, noise=noise, sigmas=sigmas, level_weights=level_weights, embed=embed, proj_in=proj_in, proj_out=proj_out, head_out=head_out, qk_gain=qk_gain)


def head_norm(acts, gain):
    spread = acts.shape[0]
    shaped = jax.nn.silu(acts).reshape(spread, HEADS, HD)
    shaped = shaped * lax.rsqrt(lax.optimization_barrier(jnp.mean(shaped * shaped, axis=-1, keepdims=True)) + 1e-06) * gain
    return shaped.astype(jnp.bfloat16)

def one_head(pieces):
    query, keys, values = pieces
    scores = jnp.dot(query, keys.T, preferred_element_type=jnp.float32) / math.sqrt(HD)
    scores = scores - lax.optimization_barrier(jnp.max(scores, axis=-1, keepdims=True))
    weights = jnp.exp(scores)
    weights = (weights / lax.optimization_barrier(jnp.sum(weights, axis=-1, keepdims=True))).astype(jnp.bfloat16)
    return jnp.dot(weights, values, preferred_element_type=jnp.float32).astype(jnp.bfloat16)

def score_net(xin, emb, pin, pout, whead, gains):
    spread = xin.shape[0]
    hidden = jnp.dot(xin, emb, preferred_element_type=jnp.float32).astype(jnp.bfloat16)
    queries = head_norm(jnp.dot(hidden, pin[0], preferred_element_type=jnp.float32), gains[0])
    keys = head_norm(jnp.dot(hidden, pin[1], preferred_element_type=jnp.float32), gains[1])
    values = jax.nn.silu(jnp.dot(hidden, pin[2], preferred_element_type=jnp.float32)).astype(jnp.bfloat16)
    values = values.reshape(spread, HEADS, HD)
    outputs = lax.map(one_head, (queries.transpose(1, 0, 2), keys.transpose(1, 0, 2), values.transpose(1, 0, 2)))
    flat = outputs.transpose(1, 0, 2).reshape(spread, HEADS * HD)
    middle = jnp.dot(flat, pout, preferred_element_type=jnp.float32)
    branch = jnp.dot(middle, whead.astype(jnp.float32), precision=lax.Precision.HIGHEST)
    return branch + jnp.dot(hidden, whead, preferred_element_type=jnp.float32)

def reference(feats, gen_gain, gen_weight, noise, sigmas, level_weights, embed, proj_in, proj_out, head_out, qk_gain):
    hidden = feats.astype(jnp.float32)
    rms = lax.rsqrt(lax.optimization_barrier(jnp.mean(hidden * hidden, axis=-1, keepdims=True)) + 1e-06)
    normed = hidden * rms
    u_mat = (normed * gen_gain).astype(jnp.bfloat16)
    flat_u = u_mat.reshape(SAMPLES * SLAB, D)
    x_zero = jnp.dot(flat_u, gen_weight, preferred_element_type=jnp.float32).reshape(SAMPLES, SLAB, C)
    total = jnp.zeros((SAMPLES, SLAB, C), jnp.float32)
    for level in range(LEVELS):
        sigma = sigmas[level]
        noisy = (x_zero + sigma * noise[level]) * lax.rsqrt(sigma * sigma + 1.0)
        noisy = noisy.astype(jnp.bfloat16)

        def per_sample(xin):
            teacher = score_net(xin, embed[0], proj_in[0], proj_out[0], head_out[0], qk_gain[0])
            faked = score_net(xin, embed[1], proj_in[1], proj_out[1], head_out[1], qk_gain[1])
            return faked - teacher
        total = total + level_weights[level] * lax.map(per_sample, noisy)
    g_low = total.astype(jnp.bfloat16).reshape(SAMPLES * SLAB, C)
    d_u = jnp.dot(g_low, gen_weight.T, preferred_element_type=jnp.float32)
    flat_norm = normed.reshape(SAMPLES * SLAB, D)
    flat_rms = rms.reshape(SAMPLES * SLAB, 1)
    d_norm = d_u * gen_gain
    inner = lax.optimization_barrier(jnp.mean(d_norm * flat_norm, axis=-1, keepdims=True))
    grad_h = (flat_rms * (d_norm - flat_norm * inner)).astype(jnp.bfloat16).reshape(SAMPLES, SLAB, D)
    factor = 1.0 / math.sqrt(SAMPLES * SLAB)
    grad_weight = jnp.dot(flat_u.T, g_low, preferred_element_type=jnp.float32) * factor
    grad_gain = lax.optimization_barrier(jnp.sum(d_u * flat_norm, axis=0)) * factor
    return (grad_h, grad_weight, grad_gain)
```

```python
import math

import jax
import jax.numpy as jnp
from jax import lax
from jax.sharding import PartitionSpec as P

HD = 128
BF = jnp.bfloat16
F32 = jnp.float32


def on_device(feats, gen_gain, gen_weight, noise, sigmas, level_weights, embed, proj_in, proj_out, head_out, qk_gain):
    span, width_d = feats.shape[1:]
    ways = lax.axis_size("seq")
    rows = span // ways
    chans = gen_weight.shape[1]
    seq = lax.axis_index("seq")
    first_row = seq * rows
    part = proj_in.shape[2]
    spot = (lax.axis_index("level") * lax.axis_size("dp") + lax.axis_index("dp")) * part
    heads = proj_in.shape[3] // HD

    emb = lax.dynamic_slice_in_dim(embed, spot, part, 2)
    head = lax.dynamic_slice_in_dim(head_out, spot, part, 1)
    entry = jnp.einsum("ncd,njdw->njcw", emb, proj_in, preferred_element_type=F32)
    leave = jnp.einsum("nwd,ndc->ncw", proj_out, head, preferred_element_type=F32)
    fused = jnp.concatenate([entry, leave[:, None]], axis=1).astype(BF)
    fused = lax.psum(fused, ("level", "dp")).astype(BF)

    hidden = feats[0]
    wide = hidden.astype(F32)
    rms = lax.rsqrt(jnp.mean(wide * wide, axis=-1, keepdims=True) + 1e-06)
    scaled = (gen_weight.astype(F32) * gen_gain[:, None]).astype(BF)
    x_zero = jnp.dot(hidden, scaled, preferred_element_type=F32) * rms
    sigma = sigmas[0]
    xin = ((x_zero + sigma * noise[0, 0]) * lax.rsqrt(sigma * sigma + 1.0)).astype(BF)

    acts = jax.nn.silu(jnp.einsum("sc,njcw->njsw", xin, fused[:, :3], preferred_element_type=F32))
    acts = acts.reshape(2, 3, span, heads, HD)
    paired = acts[:, :2]
    paired = paired * lax.rsqrt(jnp.mean(paired * paired, axis=-1, keepdims=True) + 1e-06)
    paired = (paired * qk_gain[:, :, None, None, :]).astype(BF)
    values = acts[:, 2].astype(BF)
    scores = jnp.einsum("nqhd,nkhd->nhqk", paired[:, 0], paired[:, 1], preferred_element_type=F32)
    weights = jnp.exp(scores * (1.0 / math.sqrt(HD)))
    weights = (weights / jnp.sum(weights, axis=-1, keepdims=True)).astype(BF)
    outs = jnp.einsum("nhqk,nkhd->nqhd", weights, values, preferred_element_type=F32).astype(BF)
    outs = outs.reshape(2, span, heads * HD)
    field = jnp.einsum("nsw,ncw->nsc", outs, fused[:, 3], preferred_element_type=F32)
    part_s = width_d // ways
    emb_s = lax.dynamic_slice_in_dim(embed, seq * part_s, part_s, 2)
    head_s = lax.dynamic_slice_in_dim(head_out, seq * part_s, part_s, 1)
    straight = jnp.einsum("ncd,nde->nce", emb_s, head_s, preferred_element_type=F32)
    straight = (straight[1] - straight[0]).astype(BF)
    total = field[1] - field[0] + jnp.dot(xin, straight, preferred_element_type=F32)
    total = (level_weights[0] * total).reshape(span // 2, 2 * chans)
    total = lax.psum(total, ("level", "seq")).reshape(span, chans)
    g_low = total.astype(BF)

    term = jnp.einsum("sc,sd->cd", (g_low.astype(F32) * rms).astype(BF), hidden, preferred_element_type=F32)
    wsum = lax.psum_scatter(term.astype(BF), "dp", scatter_dimension=1, tiled=True).astype(F32)
    cut = width_d // lax.axis_size("dp")
    at = lax.axis_index("dp") * cut
    gain_cut = lax.dynamic_slice_in_dim(gen_gain, at, cut, 0)
    weight_cut = lax.dynamic_slice_in_dim(gen_weight, at, cut, 0).astype(F32)
    wsum = wsum.T * (1.0 / math.sqrt(lax.axis_size("dp") * span))
    grad_gain = jnp.sum(wsum * weight_cut, axis=1)
    grad_weight = wsum * gain_cut[:, None]

    own = lambda a: lax.dynamic_slice_in_dim(a, first_row, rows, 0)
    own_g, own_rms = own(g_low), own(rms)
    inner = jnp.sum(own_g.astype(F32) * own(x_zero), axis=-1, keepdims=True) / width_d
    d_norm = jnp.dot(own_g, gen_weight.T, preferred_element_type=F32) * gen_gain
    grad_h = (own_rms * (d_norm - own(wide) * own_rms * inner)).astype(BF)
    return (grad_h[None], grad_weight, grad_gain)


def solution(mesh):
    in_specs = (
        P("dp", None, None),
        P(),
        P(),
        P("level", "dp", None, None),
        P("level"),
        P("level"),
        P(),
        P(None, None, ("level", "dp"), "seq"),
        P(None, "seq", ("level", "dp")),
        P(),
        P(),
    )
    out_specs = (P("dp", "seq", None), P("dp", None), P("dp"))
    return jax.shard_map(on_device, mesh=mesh, in_specs=in_specs, out_specs=out_specs, check_vma=False)
```

```python
import functools
import math

import jax
import jax.numpy as jnp
from jax import lax
from jax.experimental import pallas as pl
from jax.experimental.pallas import tpu as pltpu
from jax.sharding import PartitionSpec as P

HD = 128
BF = jnp.bfloat16
F32 = jnp.float32
MESH = pl.DeviceIdType.MESH
NT = (((1,), (1,)), ((), ()))
NN = (((1,), (0,)), ((), ()))
FEAT_CHUNKS = 5
QBLOCK = 256


def mm(a, b, dims=NN):
    return lax.dot_general(a, b, dims, preferred_element_type=F32)


def window(index, part):
    if part % 128 == 0:
        return index * part, part, 0
    assert part % 128 == 64
    offset = lax.rem(index, 2) * 64
    return index * part - offset, part + 64, offset


def kernel(
    sizes,
    sigma_ref, lw_ref, qk_ref, feats_hbm, gain_hbm, gw_hbm, noise_hbm, embed_hbm, pin_hbm, po_hbm, ho_hbm,
    oh_hbm, ow_hbm, og_ref,
    fbuf, gain, gw, noise, ewin, hwin, ewin_s, hwin_s, wbuf,
    wpart, rx, zpart, rz, wfull,
    ssq, x0, rms, xin, qbuf, kbuf, vext, obuf,
    tsend, b1, b2, gfull, psend, crecv, whalf, hout,
    in_sem, feat_sem, out_sem,
    s_rx, r_rx, s_rz, r_rz, s_az, r_az, s_ax, r_ax,
    s_b1, r_b1, s_b2, r_b2, s_b3, r_b3, s_c, r_c, s_k, r_k,
):
    L, S, X = sizes
    D = fbuf.shape[1]
    span = fbuf.shape[0]
    chans = gw.shape[0]
    half = span // 2
    l, s, d = lax.axis_index("level"), lax.axis_index("seq"), lax.axis_index("dp")
    core = lax.rem(s, 2)
    mate = s + 1 - 2 * core

    def remote(src, dst, ssem, rsem, where):
        copy = pltpu.make_async_remote_copy(
            src_ref=src, dst_ref=dst, send_sem=ssem, recv_sem=rsem, device_id=where, device_id_type=MESH
        )
        copy.start()
        return copy

    def drain(ref, sem):
        pltpu.make_async_copy(ref, ref, sem).wait()

    barrier = pltpu.get_barrier_semaphore()
    for o in range(1, X):
        pl.semaphore_signal(barrier, inc=1, device_id={"dp": lax.rem(d + o, X)}, device_id_type=MESH)
    for o in range(1, L):
        pl.semaphore_signal(barrier, inc=1, device_id={"level": lax.rem(l + o, L)}, device_id_type=MESH)
    for o in range(1, S):
        pl.semaphore_signal(barrier, inc=1, device_id={"seq": lax.rem(s + o, S)}, device_id_type=MESH)

    part = pin_hbm.shape[2]
    start_a, win_a, off_a = window(l * X + d, part)
    part_s = D // S
    start_s, win_s, off_s = window(s, part_s)
    if win_a != part:
        start_a = pl.multiple_of(start_a, 128)
        off_a = pl.multiple_of(off_a, 64)
    if win_s != part_s:
        start_s = pl.multiple_of(start_s, 128)
    cols_a, cols_s = pl.ds(start_a, win_a), pl.ds(start_s, win_s)
    inner_rows = pl.ds(off_a, part)

    loads = {}

    def load(name, src, dst):
        k = len(loads)
        copy = pltpu.make_async_copy(src, dst, in_sem.at[k])
        copy.start()
        loads[name] = copy

    load("e", embed_hbm.at[:, :, cols_a], ewin)
    load("p0", pin_hbm.at[0], wbuf.at[0, pl.ds(0, 3), inner_rows])
    load("h", ho_hbm.at[:, :, cols_a], hwin)
    load("o0", po_hbm.at[0], wbuf.at[0, 3, inner_rows])
    load("p1", pin_hbm.at[1], wbuf.at[1, pl.ds(0, 3), inner_rows])
    load("o1", po_hbm.at[1], wbuf.at[1, 3, inner_rows])
    load("gain", gain_hbm, gain)
    load("gw", gw_hbm, gw)
    fc = D // FEAT_CHUNKS
    for c in range(FEAT_CHUNKS):
        pltpu.make_async_copy(
            feats_hbm.at[0, :, pl.ds(c * fc, fc)], fbuf.at[:, pl.ds(c * fc, fc)], feat_sem.at[c]
        ).start()
    load("es", embed_hbm.at[:, :, cols_s], ewin_s)
    load("hs", ho_hbm.at[:, :, cols_s], hwin_s)
    load("noise", noise_hbm, noise)

    if win_a != part:
        pad = pl.ds(pl.multiple_of((part // 64) * 64 - (part // 64) * off_a, 64), 64)
        for n in range(2):
            for j in range(4):
                wbuf[n, j, pad, :] = jnp.zeros((64, wbuf.shape[3]), BF)
    for h in range(2):
        vext[h, :, HD:] = jnp.ones((span, HD), BF)

    def fuse(n):
        for j in range(4):
            left = ewin if j < 3 else hwin
            x = mm(left[n], wbuf[n, j]).astype(BF)
            wpart[n, j, 0:chans, :] = x[:, :HD]
            wpart[n, j, chans : 2 * chans, :] = x[:, HD:]

    def send_rx(n):
        for o in (2, 1, 3) if X == 4 else range(1, X):
            to = lax.rem(d + o, X)
            remote(wpart.at[n, to], rx.at[n, o - 1], s_rx.at[n], r_rx.at[n], {"dp": to})

    def turn_rx(n):
        drain(rx.at[n], r_rx.at[n])
        total = wpart[n, d].astype(F32)
        for o in range(X - 1):
            total = total + rx[n, o].astype(F32)
        zpart[n] = total.astype(BF).reshape(zpart.shape[1:])
        for o in range(L - 1, 0, -1):
            to = lax.rem(l + o, L)
            remote(zpart.at[n, to], rz.at[n, o - 1], s_rz.at[n], r_rz.at[n], {"level": to})

    zrows = 2 * chans // L
    own_z = pl.ds(pl.multiple_of(l * zrows, zrows), zrows)

    def turn_rz(n):
        drain(rz.at[n], r_rz.at[n])
        total = zpart[n, l].astype(F32)
        for o in range(L - 1):
            total = total + rz[n, o].astype(F32)
        wfull[n, d, own_z, :] = total.astype(BF)
        block = wfull.at[n, d, own_z]
        for o in range(L - 1, 0, -1):
            remote(block, block, s_az.at[n], r_az.at[n], {"level": lax.rem(l + o, L)})

    def turn_az(n):
        drain(rz.at[n], r_az.at[n])
        block = wfull.at[n, d]
        for o in (2, 1, 3) if X == 4 else range(1, X):
            remote(block, block, s_ax.at[n], r_ax.at[n], {"dp": lax.rem(d + o, X)})

    def turn_ax(n):
        drain(rx.at[n], r_ax.at[n])

    def feat_chunk(c):
        cols = pl.ds(c * fc, fc)
        pltpu.make_async_copy(feats_hbm.at[0, :, cols], fbuf.at[:, cols], feat_sem.at[c]).wait()
        scaled = (gw[:, c * fc : (c + 1) * fc].astype(F32) * gain[:, c * fc : (c + 1) * fc]).astype(BF)

        def rows_body(i, _):
            rows = pl.ds(pl.multiple_of(i * 64, 64), 64)
            acc = jnp.zeros((64, 128), F32)
            for k in range(fc // 128):
                x = fbuf[rows, c * fc + k * 128 : c * fc + (k + 1) * 128].astype(F32)
                acc = acc + x * x
            ssq[rows, :] = acc if c == 0 else ssq[rows, :] + acc
            return 0

        lax.fori_loop(0, span // 64, rows_body, 0)
        prod = mm(fbuf[:, c * fc : (c + 1) * fc], scaled, NT)
        x0[...] = prod if c == 0 else x0[...] + prod

    loads["e"].wait()
    loads["h"].wait()
    loads["p0"].wait()
    loads["o0"].wait()
    fuse(0)
    pl.semaphore_wait(barrier, X + L + S - 3)
    send_rx(0)
    loads["p1"].wait()
    loads["o1"].wait()
    fuse(1)
    send_rx(1)
    loads["gain"].wait()
    loads["gw"].wait()
    feat_chunk(0)
    turn_rx(0)
    feat_chunk(1)
    turn_rx(1)
    turn_rz(0)
    feat_chunk(2)
    turn_rz(1)
    turn_az(0)
    feat_chunk(3)
    turn_az(1)
    feat_chunk(4)

    loads["noise"].wait()
    loads["es"].wait()
    loads["hs"].wait()
    scale = lax.rsqrt(jnp.sum(ssq[...], axis=-1, keepdims=True) * (1.0 / D) + 1e-06)
    rms[...] = jnp.broadcast_to(scale, rms.shape)
    xz = x0[...] * scale
    x0[...] = xz
    sig = jnp.full((1, chans), sigma_ref[0], F32)
    xin[...] = ((xz + sig * noise[...].T) * lax.rsqrt(sig * sig + 1.0)).astype(BF)

    def straight(n):
        e = ewin_s[n]
        if win_s != part_s:
            lane = lax.broadcasted_iota(jnp.int32, (chans, win_s), 1)
            keep = jnp.logical_and(lane >= off_s, lane < off_s + part_s)
            e = jnp.where(keep, e.astype(F32), 0.0).astype(BF)
        return mm(hwin_s[n], e, NT)

    bent = (straight(1) - straight(0)).astype(BF)
    none = jnp.zeros_like(bent)

    def packed(left, rightT):
        blank = jnp.zeros_like(rightT)
        low = mm(left[:half], jnp.concatenate([rightT, blank], axis=0), NT)
        return low + mm(left[half:], jnp.concatenate([blank, rightT], axis=0), NT)

    total = packed(xin[...], bent)

    fold = math.log2(math.e) / math.sqrt(HD)
    for n in range(2):
        turn_ax(n)
        mats = [jnp.concatenate([wfull[n, j, :chans], wfull[n, j, chans:]], axis=1) for j in range(4)]

        def rows_body(i, _, n=n, mats=mats):
            rows = pl.ds(pl.multiple_of(i * 128, 128), 128)
            x = xin[rows, :]
            for j in range(3):
                a = mm(x, mats[j]) * 0.5
                act = a * jnp.tanh(a) + a
                for h in range(2):
                    t = act[:, h * HD : (h + 1) * HD]
                    if j == 2:
                        vext[h, rows, 0:HD] = t.astype(BF)
                        continue
                    mean = jnp.mean(t * t, axis=-1, keepdims=True)
                    row = qk_ref[2 * n + j : 2 * n + j + 1, :]
                    if j == 0:
                        row = row * fold
                    t = (t * lax.rsqrt(mean + 1e-06) * row).astype(BF)
                    if j == 0:
                        qbuf[h, rows, :] = t
                    else:
                        kbuf[h, rows, :] = t
            return 0

        lax.fori_loop(0, span // 128, rows_body, 0)
        for b in range(span // QBLOCK):
            rows = slice(b * QBLOCK, (b + 1) * QBLOCK)
            for h in range(2):
                weights = jnp.exp2(mm(qbuf[h, rows, :], kbuf[h], NT)).astype(BF)
                both = mm(weights, vext[h])
                obuf[rows, h * HD : (h + 1) * HD] = (both[:, :HD] / both[:, HD:]).astype(BF)
        field = packed(obuf[...], mats[3])
        total = total + field if n else total - field

    tsend[...] = (total * lw_ref[0]).astype(BF)
    trows = half // S

    def chunk(i):
        return pl.ds(pl.multiple_of(i * trows, trows), trows)

    for o in range(1, S):
        to = lax.rem(s + o, S)
        remote(tsend.at[chunk(to)], b1.at[o - 1], s_b1, r_b1, {"seq": to})
    drain(b1, r_b1)
    acc = tsend[chunk(s), :].astype(F32)
    for o in range(S - 1):
        acc = acc + b1[o].astype(F32)
    b2[l] = acc
    for o in range(1, L):
        remote(b2.at[l], b2.at[l], s_b2, r_b2, {"level": lax.rem(l + o, L)})
    drain(b2.at[pl.ds(0, L - 1)], r_b2)
    acc = b2[0]
    for i in range(1, L):
        acc = acc + b2[i]
    gfull[chunk(s), :] = acc.astype(BF)
    for o in range(1, S):
        remote(gfull.at[chunk(s)], gfull.at[chunk(s)], s_b3, r_b3, {"seq": lax.rem(s + o, S)})
    drain(b1, r_b3)

    cut = D // X
    side = cut // 2
    lane = lax.broadcasted_iota(jnp.int32, (half, 2 * chans), 1)
    scaling = jnp.where(lane < chans, rms[0:half, :], rms[half:, :])
    turned = (gfull[...].astype(F32) * scaling).T.astype(BF)
    for o in ((2, 1, 3) if X == 4 else tuple(range(1, X))) + (0,):
        to = lax.rem(d + o, X)
        cols = pl.ds(pl.multiple_of(to * cut + core * side, 128), side)
        term = mm(turned[:chans], fbuf[0:half, cols]) + mm(turned[chans:], fbuf[half:, cols])
        if o:
            psend[o - 1] = term.astype(BF)
            remote(psend.at[o - 1], crecv.at[d], s_c, r_c, {"dp": to})
        else:
            crecv[d] = term.astype(BF)

    rows_h = span // S
    first = s * rows_h
    which = first // half
    own = pl.ds(pl.multiple_of(first, rows_h), rows_h)
    g_own = gfull[pl.ds(pl.multiple_of(first - which * half, rows_h), rows_h), :].astype(F32)
    g_own = jnp.where(which == 0, g_own, pltpu.roll(g_own, chans, 1))[:, :chans]
    inner = jnp.sum(g_own * x0[own, :], axis=-1, keepdims=True) * (1.0 / D)
    scale_own = rms[own, 0:1]
    lessen = scale_own * inner
    g_own = g_own.astype(BF)
    for c in range(FEAT_CHUNKS):
        cols = slice(c * fc, (c + 1) * fc)
        grad = mm(g_own, gw[:, cols]) * gain[:, cols] - fbuf[own, cols].astype(F32) * lessen
        hout[:, cols] = (grad * scale_own).astype(BF)
    send_h = pltpu.make_async_copy(hout, oh_hbm.at[0], out_sem.at[0])
    send_h.start()

    drain(crecv.at[pl.ds(0, X - 1)], r_c)
    acc = crecv[0].astype(F32)
    for i in range(1, X):
        acc = acc + crecv[i].astype(F32)
    factor = 1.0 / math.sqrt(X * span)
    mine = pl.ds(pl.multiple_of(d * cut + core * side, 128), side)
    whalf[core] = acc * (gain[:, mine] * factor)
    remote(whalf.at[core], whalf.at[core], s_k, r_k, {"seq": mate})
    spot = pl.ds(pl.multiple_of(core * side, 128), side)
    send_a = pltpu.make_async_copy(whalf.at[core], ow_hbm.at[:, spot], out_sem.at[1])
    send_a.start()

    drain(psend, s_c)
    for n in range(2):
        drain(rx.at[n], s_rx.at[n])
        drain(rz.at[n], s_rz.at[n])
        drain(rz.at[n], s_az.at[n])
        drain(rx.at[n], s_ax.at[n])
    drain(b1, s_b1)
    drain(b2.at[pl.ds(0, L - 1)], s_b2)
    drain(b1, s_b3)

    drain(whalf.at[0], r_k)
    spot_b = pl.ds(pl.multiple_of((1 - core) * side, 128), side)
    send_b = pltpu.make_async_copy(whalf.at[1 - core], ow_hbm.at[:, spot_b], out_sem.at[2])
    send_b.start()
    for i in range(2):
        cols = pl.ds(pl.multiple_of(d * cut + i * side, 128), side)
        inside = jnp.sum(whalf[i] * gw[:, cols].astype(F32), axis=0, keepdims=True)
        og_ref[:, i * side : (i + 1) * side] = inside / gain[:, cols]
    drain(whalf.at[0], s_k)
    send_h.wait()
    send_a.wait()
    send_b.wait()


def on_device(feats, gen_gain, gen_weight, noise, sigmas, level_weights, embed, proj_in, proj_out, head_out, qk_gain):
    sizes = L, S, X = tuple(lax.axis_size(a) for a in ("level", "seq", "dp"))
    span, D = feats.shape[1:]
    chans = gen_weight.shape[1]
    part = proj_in.shape[2]
    win_a = part if part % 128 == 0 else part + 64
    win_s = D // S if D // S % 128 == 0 else D // S + 64
    half = span // 2
    side = D // X // 2
    rows_h = span // S
    hbm = pl.BlockSpec(memory_space=pl.ANY)
    vmem = pl.BlockSpec(memory_space=pltpu.VMEM)
    smem = pl.BlockSpec(memory_space=pltpu.SMEM)
    V = pltpu.VMEM
    dma = pltpu.SemaphoreType.DMA
    scratch = [
        V((span, D), BF), V((1, D), F32), V((chans, D), BF), V((chans, span), F32),
        V((2, chans, win_a), BF), V((2, chans, win_a), BF), V((2, chans, win_s), BF), V((2, chans, win_s), BF),
        V((2, 4, win_a, 2 * HD), BF),
        V((2, 4, 2 * chans, HD), BF), V((2, X - 1, 2 * chans, HD), BF),
        V((2, L, 2 * chans // L, HD), BF), V((2, L - 1, 2 * chans // L, HD), BF),
        V((2, 4, 2 * chans, HD), BF),
        V((span, 128), F32), V((span, chans), F32), V((span, 128), F32), V((span, chans), BF),
        V((2, span, HD), BF), V((2, span, HD), BF), V((2, span, 2 * HD), BF), V((span, 2 * HD), BF),
        V((half, 2 * chans), BF), V((S - 1, half // S, 2 * chans), BF), V((L, half // S, 2 * chans), F32),
        V((half, 2 * chans), BF), V((X - 1, chans, side), BF), V((X, chans, side), BF), V((2, chans, side), F32),
        V((rows_h, D), BF),
        dma((11,)), dma((FEAT_CHUNKS,)), dma((3,)),
    ] + [dma((2,))] * 8 + [dma] * 10
    out_h, out_w, out_g = pl.pallas_call(
        functools.partial(kernel, sizes),
        out_shape=(
            jax.ShapeDtypeStruct((1, rows_h, D), BF),
            jax.ShapeDtypeStruct((chans, 2 * side), F32),
            jax.ShapeDtypeStruct((1, 2 * side), F32),
        ),
        in_specs=[smem, smem, vmem] + [hbm] * 8,
        out_specs=(hbm, hbm, vmem),
        scratch_shapes=scratch,
        compiler_params=pltpu.CompilerParams(
            collective_id=0, has_side_effects=True, vmem_limit_bytes=56 * 1024 * 1024
        ),
    )(
        sigmas, level_weights, qk_gain.reshape(4, HD), feats, gen_gain[None], gen_weight.T, noise[0, 0].T,
        embed, proj_in, jnp.swapaxes(proj_out, 1, 2), jnp.swapaxes(head_out, 1, 2),
    )
    return out_h, out_w.T, out_g[0]


def solution(mesh):
    in_specs = (
        P("dp", None, None),
        P(),
        P(),
        P("level", "dp", None, None),
        P("level"),
        P("level"),
        P(),
        P(None, None, ("level", "dp"), "seq"),
        P(None, "seq", ("level", "dp")),
        P(),
        P(),
    )
    out_specs = (P("dp", "seq", None), P("dp", None), P("dp"))
    return jax.shard_map(on_device, mesh=mesh, in_specs=in_specs, out_specs=out_specs, check_vma=False)
```

```python
import functools
import math

import jax
import jax.numpy as jnp
from jax import lax
from jax.experimental import pallas as pl
from jax.experimental.pallas import tpu as pltpu
from jax.sharding import PartitionSpec as P

HD = 128
BF = jnp.bfloat16
F32 = jnp.float32
MESH = pl.DeviceIdType.MESH
NT = (((1,), (1,)), ((), ()))
NN = (((1,), (0,)), ((), ()))
FEAT_CHUNKS = 5
QBLOCK = 256


def mm(a, b, dims=NN):
    return lax.dot_general(a, b, dims, preferred_element_type=F32)


def window(index, part):
    if part % 128 == 0:
        return index * part, part, 0
    assert part % 128 == 64
    offset = lax.rem(index, 2) * 64
    return index * part - offset, part + 64, offset


def kernel(
    sizes,
    sigma_ref, lw_ref, qk_ref, feats_hbm, gain_hbm, gw_hbm, noise_hbm, embed_hbm, pin_hbm, po_hbm, ho_hbm,
    oh_hbm, ow_hbm, og_ref,
    fbuf, gain, gw, noise, ewin, hwin, ewin_s, hwin_s, wbuf,
    wpart, rx, wfull,
    ssq, x0, rms, xin, qbuf, kbuf, vext, obuf,
    tsend, b1, b2, gfull, psend, crecv, whalf, hout,
    in_sem, feat_sem, out_sem,
    s_rx, r_rx, s_ax, r_ax,
    s_b1, r_b1, s_b2, r_b2, s_b3, r_b3, s_c, r_c, s_k, r_k,
):
    L, S, X = sizes
    D = fbuf.shape[1]
    span = fbuf.shape[0]
    chans = gw.shape[0]
    half = span // 2
    l, s, d = lax.axis_index("level"), lax.axis_index("seq"), lax.axis_index("dp")
    core = lax.rem(s, 2)
    mate = s + 1 - 2 * core

    team = [
        {"level": lax.rem(l + a, L), "dp": lax.rem(d + b, X)} for a in range(L) for b in range(X) if a or b
    ]
    pairs = S // 2
    chips = L * pairs

    def chip(i):
        return {"level": lax.rem(l + i % L, L), "seq": 2 * lax.rem(s // 2 + i // L, pairs) + core}

    def remote(src, dst, ssem, rsem, where):
        copy = pltpu.make_async_remote_copy(
            src_ref=src, dst_ref=dst, send_sem=ssem, recv_sem=rsem, device_id=where, device_id_type=MESH
        )
        copy.start()
        return copy

    def drain(ref, sem):
        pltpu.make_async_copy(ref, ref, sem).wait()

    barrier = pltpu.get_barrier_semaphore()
    for peer in team + [chip(i) for i in range(1, chips)] + [{"seq": mate}]:
        pl.semaphore_signal(barrier, inc=1, device_id=peer, device_id_type=MESH)

    part = pin_hbm.shape[2]
    start_a, win_a, off_a = window(l * X + d, part)
    part_s = D // S
    start_s, win_s, off_s = window(s, part_s)
    if win_a != part:
        start_a = pl.multiple_of(start_a, 128)
        off_a = pl.multiple_of(off_a, 64)
    if win_s != part_s:
        start_s = pl.multiple_of(start_s, 128)
    cols_a, cols_s = pl.ds(start_a, win_a), pl.ds(start_s, win_s)
    inner_rows = pl.ds(off_a, part)

    loads = {}

    def load(name, src, dst):
        k = len(loads)
        copy = pltpu.make_async_copy(src, dst, in_sem.at[k])
        copy.start()
        loads[name] = copy

    load("e", embed_hbm.at[:, :, cols_a], ewin)
    load("p0", pin_hbm.at[0], wbuf.at[0, pl.ds(0, 3), inner_rows])
    load("h", ho_hbm.at[:, :, cols_a], hwin)
    load("o0", po_hbm.at[0], wbuf.at[0, 3, inner_rows])
    load("p1", pin_hbm.at[1], wbuf.at[1, pl.ds(0, 3), inner_rows])
    load("o1", po_hbm.at[1], wbuf.at[1, 3, inner_rows])
    load("gain", gain_hbm, gain)
    load("gw", gw_hbm, gw)
    fc = D // FEAT_CHUNKS
    for c in range(FEAT_CHUNKS):
        pltpu.make_async_copy(
            feats_hbm.at[0, :, pl.ds(c * fc, fc)], fbuf.at[:, pl.ds(c * fc, fc)], feat_sem.at[c]
        ).start()
    load("es", embed_hbm.at[:, :, cols_s], ewin_s)
    load("hs", ho_hbm.at[:, :, cols_s], hwin_s)
    load("noise", noise_hbm, noise)

    if win_a != part:
        pad = pl.ds(pl.multiple_of((part // 64) * 64 - (part // 64) * off_a, 64), 64)
        for n in range(2):
            for j in range(4):
                wbuf[n, j, pad, :] = jnp.zeros((64, wbuf.shape[3]), BF)
    for h in range(2):
        vext[h, :, HD:] = jnp.ones((span, HD), BF)

    def fuse(n):
        for j in range(4):
            left = ewin if j < 3 else hwin
            x = mm(left[n], wbuf[n, j]).astype(BF)
            base = 2 * j * chans
            wpart[n, base : base + chans, :] = x[:, :HD]
            wpart[n, base + chans : base + 2 * chans, :] = x[:, HD:]

    share = 8 * chans // (L * X)

    def share_rows(peer):
        return pl.ds(pl.multiple_of((peer["level"] * X + peer["dp"]) * share, share), share)

    own_share = share_rows({"level": l, "dp": d})

    def send_shares(n):
        for o, peer in enumerate(team):
            remote(wpart.at[n, share_rows(peer)], rx.at[n, o], s_rx.at[n], r_rx.at[n], peer)

    def sum_shares(n):
        drain(rx.at[n], r_rx.at[n])
        total = wpart[n, own_share, :].astype(F32)
        for o in range(len(team)):
            total = total + rx[n, o].astype(F32)
        wfull[n, own_share, :] = total.astype(BF)
        for peer in team:
            remote(wfull.at[n, own_share], wfull.at[n, own_share], s_ax.at[n], r_ax.at[n], peer)

    def feat_chunk(c):
        cols = pl.ds(c * fc, fc)
        pltpu.make_async_copy(feats_hbm.at[0, :, cols], fbuf.at[:, cols], feat_sem.at[c]).wait()
        scaled = (gw[:, c * fc : (c + 1) * fc].astype(F32) * gain[:, c * fc : (c + 1) * fc]).astype(BF)

        def rows_body(i, _):
            rows = pl.ds(pl.multiple_of(i * 64, 64), 64)
            acc = jnp.zeros((64, 128), F32)
            for k in range(fc // 128):
                x = fbuf[rows, c * fc + k * 128 : c * fc + (k + 1) * 128].astype(F32)
                acc = acc + x * x
            ssq[rows, :] = acc if c == 0 else ssq[rows, :] + acc
            return 0

        lax.fori_loop(0, span // 64, rows_body, 0)
        prod = mm(fbuf[:, c * fc : (c + 1) * fc], scaled, NT)
        x0[...] = prod if c == 0 else x0[...] + prod

    loads["e"].wait()
    loads["h"].wait()
    loads["p0"].wait()
    loads["o0"].wait()
    fuse(0)
    loads["p1"].wait()
    loads["o1"].wait()
    fuse(1)
    loads["gain"].wait()
    loads["gw"].wait()
    feat_chunk(0)
    feat_chunk(1)
    pl.semaphore_wait(barrier, L * X + chips - 1)
    send_shares(0)
    send_shares(1)
    for c in range(2, FEAT_CHUNKS):
        feat_chunk(c)

    loads["noise"].wait()
    loads["es"].wait()
    loads["hs"].wait()
    scale = lax.rsqrt(jnp.sum(ssq[...], axis=-1, keepdims=True) * (1.0 / D) + 1e-06)
    rms[...] = jnp.broadcast_to(scale, rms.shape)
    xz = x0[...] * scale
    x0[...] = xz
    sig = jnp.full((1, chans), sigma_ref[0], F32)
    xin[...] = ((xz + sig * noise[...].T) * lax.rsqrt(sig * sig + 1.0)).astype(BF)

    def straight(n):
        e = ewin_s[n]
        if win_s != part_s:
            lane = lax.broadcasted_iota(jnp.int32, (chans, win_s), 1)
            keep = jnp.logical_and(lane >= off_s, lane < off_s + part_s)
            e = jnp.where(keep, e.astype(F32), 0.0).astype(BF)
        return mm(hwin_s[n], e, NT)

    bent = (straight(1) - straight(0)).astype(BF)
    none = jnp.zeros_like(bent)

    def packed(left, rightT):
        blank = jnp.zeros_like(rightT)
        low = mm(left[:half], jnp.concatenate([rightT, blank], axis=0), NT)
        return low + mm(left[half:], jnp.concatenate([blank, rightT], axis=0), NT)

    sum_shares(0)
    sum_shares(1)
    total = packed(xin[...], bent)

    fold = math.log2(math.e) / math.sqrt(HD)
    for n in range(2):
        drain(rx.at[n], r_ax.at[n])
        mats = [
            jnp.concatenate([wfull[n, (2 * j + h) * chans : (2 * j + h + 1) * chans] for h in range(2)], axis=1)
            for j in range(4)
        ]

        def rows_body(i, _, n=n, mats=mats):
            rows = pl.ds(pl.multiple_of(i * 128, 128), 128)
            x = xin[rows, :]
            for j in range(3):
                a = mm(x, mats[j]) * 0.5
                act = a * jnp.tanh(a) + a
                for h in range(2):
                    t = act[:, h * HD : (h + 1) * HD]
                    if j == 2:
                        vext[h, rows, 0:HD] = t.astype(BF)
                        continue
                    mean = jnp.mean(t * t, axis=-1, keepdims=True)
                    row = qk_ref[2 * n + j : 2 * n + j + 1, :]
                    if j == 0:
                        row = row * fold
                    t = (t * lax.rsqrt(mean + 1e-06) * row).astype(BF)
                    if j == 0:
                        qbuf[h, rows, :] = t
                    else:
                        kbuf[h, rows, :] = t
            return 0

        lax.fori_loop(0, span // 128, rows_body, 0)
        for b in range(span // QBLOCK):
            rows = slice(b * QBLOCK, (b + 1) * QBLOCK)
            for h in range(2):
                weights = jnp.exp2(mm(qbuf[h, rows, :], kbuf[h], NT)).astype(BF)
                both = mm(weights, vext[h])
                obuf[rows, h * HD : (h + 1) * HD] = (both[:, :HD] / both[:, HD:]).astype(BF)
        field = packed(obuf[...], mats[3])
        total = total + field if n else total - field

    tsend[...] = (total * lw_ref[0]).astype(BF)
    blocks = L * pairs // 2
    trows = half // blocks

    def block_of(peer):
        return pl.ds(pl.multiple_of((peer["seq"] // 4 * L + peer["level"]) * trows, trows), trows)

    me = {"level": l, "seq": s}
    spot_b = s // 2 * L + l
    b1[spot_b] = tsend[block_of(me), :]
    for i in range(1, chips):
        peer = chip(i)
        remote(tsend.at[block_of(peer)], b1.at[spot_b], s_b1, r_b1, peer)
    drain(b1.at[pl.ds(0, chips - 1)], r_b1)
    acc = b1[0].astype(F32)
    for i in range(1, chips):
        acc = acc + b1[i].astype(F32)
    b2[core] = acc
    remote(b2.at[core], b2.at[core], s_b2, r_b2, {"seq": mate})
    drain(b2.at[0], r_b2)
    mine_b = block_of(me)
    gfull[mine_b, :] = (b2[0] + b2[1]).astype(BF)
    near = [
        {"level": lax.rem(l + i % L, L), "seq": lax.rem(s + 4 * (i // L), S)} for i in range(1, blocks)
    ]
    for peer in near:
        remote(gfull.at[mine_b], gfull.at[mine_b], s_b3, r_b3, peer)
    drain(b1.at[pl.ds(0, blocks - 1)], r_b3)

    cut = D // X
    side = cut // 2
    lane = lax.broadcasted_iota(jnp.int32, (half, 2 * chans), 1)
    scaling = jnp.where(lane < chans, rms[0:half, :], rms[half:, :])
    turned = (gfull[...].astype(F32) * scaling).T.astype(BF)
    for o in ((2, 1, 3) if X == 4 else tuple(range(1, X))) + (0,):
        to = lax.rem(d + o, X)
        cols = pl.ds(pl.multiple_of(to * cut + core * side, 128), side)
        term = mm(turned[:chans], fbuf[0:half, cols]) + mm(turned[chans:], fbuf[half:, cols])
        if o:
            psend[o - 1] = term.astype(BF)
            remote(psend.at[o - 1], crecv.at[d], s_c, r_c, {"dp": to})
        else:
            crecv[d] = term.astype(BF)

    rows_h = span // S
    first = s * rows_h
    which = first // half
    own = pl.ds(pl.multiple_of(first, rows_h), rows_h)
    g_own = gfull[pl.ds(pl.multiple_of(first - which * half, rows_h), rows_h), :].astype(F32)
    g_own = jnp.where(which == 0, g_own, pltpu.roll(g_own, chans, 1))[:, :chans]
    inner = jnp.sum(g_own * x0[own, :], axis=-1, keepdims=True) * (1.0 / D)
    scale_own = rms[own, 0:1]
    lessen = scale_own * inner
    g_own = g_own.astype(BF)
    for c in range(FEAT_CHUNKS):
        cols = slice(c * fc, (c + 1) * fc)
        grad = mm(g_own, gw[:, cols]) * gain[:, cols] - fbuf[own, cols].astype(F32) * lessen
        hout[:, cols] = (grad * scale_own).astype(BF)
    send_h = pltpu.make_async_copy(hout, oh_hbm.at[0], out_sem.at[0])
    send_h.start()

    drain(crecv.at[pl.ds(0, X - 1)], r_c)
    acc = crecv[0].astype(F32)
    for i in range(1, X):
        acc = acc + crecv[i].astype(F32)
    factor = 1.0 / math.sqrt(X * span)
    mine = pl.ds(pl.multiple_of(d * cut + core * side, 128), side)
    whalf[core] = acc * (gain[:, mine] * factor)
    remote(whalf.at[core], whalf.at[core], s_k, r_k, {"seq": mate})
    spot = pl.ds(pl.multiple_of(core * side, 128), side)
    send_a = pltpu.make_async_copy(whalf.at[core], ow_hbm.at[:, spot], out_sem.at[1])
    send_a.start()

    drain(psend, s_c)
    for n in range(2):
        drain(rx.at[n], s_rx.at[n])
        drain(rx.at[n], s_ax.at[n])
    drain(b1.at[pl.ds(0, chips - 1)], s_b1)
    drain(b2.at[0], s_b2)
    drain(b1.at[pl.ds(0, blocks - 1)], s_b3)

    drain(whalf.at[0], r_k)
    spot_o = pl.ds(pl.multiple_of((1 - core) * side, 128), side)
    send_b = pltpu.make_async_copy(whalf.at[1 - core], ow_hbm.at[:, spot_o], out_sem.at[2])
    send_b.start()
    for i in range(2):
        cols = pl.ds(pl.multiple_of(d * cut + i * side, 128), side)
        inside = jnp.sum(whalf[i] * gw[:, cols].astype(F32), axis=0, keepdims=True)
        og_ref[:, i * side : (i + 1) * side] = inside / gain[:, cols]
    drain(whalf.at[0], s_k)
    send_h.wait()
    send_a.wait()
    send_b.wait()


def on_device(feats, gen_gain, gen_weight, noise, sigmas, level_weights, embed, proj_in, proj_out, head_out, qk_gain):
    sizes = L, S, X = tuple(lax.axis_size(a) for a in ("level", "seq", "dp"))
    span, D = feats.shape[1:]
    chans = gen_weight.shape[1]
    part = proj_in.shape[2]
    win_a = part if part % 128 == 0 else part + 64
    win_s = D // S if D // S % 128 == 0 else D // S + 64
    half = span // 2
    side = D // X // 2
    rows_h = span // S
    hbm = pl.BlockSpec(memory_space=pl.ANY)
    vmem = pl.BlockSpec(memory_space=pltpu.VMEM)
    smem = pl.BlockSpec(memory_space=pltpu.SMEM)
    V = pltpu.VMEM
    dma = pltpu.SemaphoreType.DMA
    scratch = [
        V((span, D), BF), V((1, D), F32), V((chans, D), BF), V((chans, span), F32),
        V((2, chans, win_a), BF), V((2, chans, win_a), BF), V((2, chans, win_s), BF), V((2, chans, win_s), BF),
        V((2, 4, win_a, 2 * HD), BF),
        V((2, 8 * chans, HD), BF), V((2, L * X - 1, 8 * chans // (L * X), HD), BF), V((2, 8 * chans, HD), BF),
        V((span, 128), F32), V((span, chans), F32), V((span, 128), F32), V((span, chans), BF),
        V((2, span, HD), BF), V((2, span, HD), BF), V((2, span, 2 * HD), BF), V((span, 2 * HD), BF),
        V((half, 2 * chans), BF), V((L * S // 2, 4 * half // (L * S), 2 * chans), BF),
        V((2, 4 * half // (L * S), 2 * chans), F32),
        V((half, 2 * chans), BF), V((X - 1, chans, side), BF), V((X, chans, side), BF), V((2, chans, side), F32),
        V((rows_h, D), BF),
        dma((11,)), dma((FEAT_CHUNKS,)), dma((3,)),
    ] + [dma((2,))] * 4 + [dma] * 10
    out_h, out_w, out_g = pl.pallas_call(
        functools.partial(kernel, sizes),
        out_shape=(
            jax.ShapeDtypeStruct((1, rows_h, D), BF),
            jax.ShapeDtypeStruct((chans, 2 * side), F32),
            jax.ShapeDtypeStruct((1, 2 * side), F32),
        ),
        in_specs=[smem, smem, vmem] + [hbm] * 8,
        out_specs=(hbm, hbm, vmem),
        scratch_shapes=scratch,
        compiler_params=pltpu.CompilerParams(
            collective_id=0, has_side_effects=True, vmem_limit_bytes=56 * 1024 * 1024
        ),
    )(
        sigmas, level_weights, qk_gain.reshape(4, HD), feats, gen_gain[None], gen_weight.T, noise[0, 0].T,
        embed, proj_in, jnp.swapaxes(proj_out, 1, 2), jnp.swapaxes(head_out, 1, 2),
    )
    return out_h, out_w.T, out_g[0]


def solution(mesh):
    in_specs = (
        P("dp", None, None),
        P(),
        P(),
        P("level", "dp", None, None),
        P("level"),
        P("level"),
        P(),
        P(None, None, ("level", "dp"), "seq"),
        P(None, "seq", ("level", "dp")),
        P(),
        P(),
    )
    out_specs = (P("dp", "seq", None), P("dp", None), P("dp"))
    return jax.shard_map(on_device, mesh=mesh, in_specs=in_specs, out_specs=out_specs, check_vma=False)
```

```python
import functools
import math

import jax
import jax.numpy as jnp
from jax import lax
from jax.experimental import pallas as pl
from jax.experimental.pallas import tpu as pltpu
from jax.sharding import PartitionSpec as P

HD = 128
BF = jnp.bfloat16
F32 = jnp.float32
MESH = pl.DeviceIdType.MESH
NT = (((1,), (1,)), ((), ()))
NN = (((1,), (0,)), ((), ()))
FEAT_CHUNKS = 5
QBLOCK = 256


def mm(a, b, dims=NN):
    return lax.dot_general(a, b, dims, preferred_element_type=F32)


def window(index, part):
    if part % 128 == 0:
        return index * part, part, 0
    assert part % 128 == 64
    offset = lax.rem(index, 2) * 64
    return index * part - offset, part + 64, offset


def kernel(
    sizes,
    sigma_ref, lw_ref, qk_hbm, feats_hbm, gain_hbm, gw_hbm, noise_hbm, embed_hbm, pin_hbm, po_hbm, ho_hbm,
    oh_ref, ow_ref, og_ref,
    qk_ref, fbuf, gain, gw, noise, ewin, hwin, ewin_s, hwin_s, wbuf,
    wpart, rx, wfull,
    ssq, x0, rms, xin, qbuf, kbuf, vext, obuf,
    tsend, b1, b2, gfull, psend, crecv,
    in_sem, feat_sem,
    s_rx, r_rx, s_ax, r_ax,
    s_b1, r_b1, s_b2, r_b2, s_b3, r_b3, s_c, r_c, s_k, r_k,
):
    L, S, X = sizes
    D = fbuf.shape[1]
    span = fbuf.shape[0]
    chans = gw.shape[0]
    half = span // 2
    l, s, d = lax.axis_index("level"), lax.axis_index("seq"), lax.axis_index("dp")
    core = lax.rem(s, 2)
    mate = s + 1 - 2 * core

    team = [
        {"level": lax.rem(l + a, L), "dp": lax.rem(d + b, X)} for a in range(L) for b in range(X) if a or b
    ]
    pairs = S // 2
    chips = L * pairs

    def chip(i):
        return {"level": lax.rem(l + i % L, L), "seq": 2 * lax.rem(s // 2 + i // L, pairs) + core}

    def remote(src, dst, ssem, rsem, where):
        copy = pltpu.make_async_remote_copy(
            src_ref=src, dst_ref=dst, send_sem=ssem, recv_sem=rsem, device_id=where, device_id_type=MESH
        )
        copy.start()
        return copy

    def drain(ref, sem):
        pltpu.make_async_copy(ref, ref, sem).wait()

    barrier = pltpu.get_barrier_semaphore()
    for peer in team + [chip(i) for i in range(1, chips)] + [{"seq": mate}]:
        pl.semaphore_signal(barrier, inc=1, device_id=peer, device_id_type=MESH)

    part = pin_hbm.shape[2]
    start_a, win_a, off_a = window(l * X + d, part)
    part_s = D // S
    start_s, win_s, off_s = window(s, part_s)
    if win_a != part:
        start_a = pl.multiple_of(start_a, 128)
        off_a = pl.multiple_of(off_a, 64)
    if win_s != part_s:
        start_s = pl.multiple_of(start_s, 128)
    cols_a, cols_s = pl.ds(start_a, win_a), pl.ds(start_s, win_s)
    inner_rows = pl.ds(off_a, part)

    loads = {}

    def load(name, src, dst):
        k = len(loads)
        copy = pltpu.make_async_copy(src, dst, in_sem.at[k])
        copy.start()
        loads[name] = copy

    load("e", embed_hbm.at[:, :, cols_a], ewin)
    load("p0", pin_hbm.at[0], wbuf.at[0, pl.ds(0, 3), inner_rows])
    load("h", ho_hbm.at[:, :, cols_a], hwin)
    load("o0", po_hbm.at[0], wbuf.at[0, 3, inner_rows])
    load("p1", pin_hbm.at[1], wbuf.at[1, pl.ds(0, 3), inner_rows])
    load("o1", po_hbm.at[1], wbuf.at[1, 3, inner_rows])
    load("gain", gain_hbm, gain)
    load("gw", gw_hbm, gw)
    fc = D // FEAT_CHUNKS
    for c in range(FEAT_CHUNKS):
        pltpu.make_async_copy(
            feats_hbm.at[0, :, pl.ds(c * fc, fc)], fbuf.at[:, pl.ds(c * fc, fc)], feat_sem.at[c]
        ).start()
    load("es", embed_hbm.at[:, :, cols_s], ewin_s)
    load("hs", ho_hbm.at[:, :, cols_s], hwin_s)
    load("noise", noise_hbm, noise)
    load("qk", qk_hbm, qk_ref)

    if win_a != part:
        pad = pl.ds(pl.multiple_of((part // 64) * 64 - (part // 64) * off_a, 64), 64)
        for n in range(2):
            for j in range(4):
                wbuf[n, j, pad, :] = jnp.zeros((64, wbuf.shape[3]), BF)
    for h in range(2):
        vext[h, :, HD:] = jnp.ones((span, HD), BF)

    def fuse(n):
        for j in range(4):
            left = ewin if j < 3 else hwin
            x = mm(left[n], wbuf[n, j]).astype(BF)
            base = 2 * j * chans
            wpart[n, base : base + chans, :] = x[:, :HD]
            wpart[n, base + chans : base + 2 * chans, :] = x[:, HD:]

    share = 8 * chans // (L * X)

    def share_rows(peer):
        return pl.ds(pl.multiple_of((peer["level"] * X + peer["dp"]) * share, share), share)

    own_share = share_rows({"level": l, "dp": d})

    def send_shares(n):
        for o, peer in enumerate(team):
            remote(wpart.at[n, share_rows(peer)], rx.at[n, o], s_rx.at[n], r_rx.at[n], peer)

    def sum_shares(n):
        drain(rx.at[n], r_rx.at[n])
        total = wpart[n, own_share, :].astype(F32)
        for o in range(len(team)):
            total = total + rx[n, o].astype(F32)
        wfull[n, own_share, :] = total.astype(BF)
        for peer in team:
            remote(wfull.at[n, own_share], wfull.at[n, own_share], s_ax.at[n], r_ax.at[n], peer)

    def feat_chunk(c):
        cols = pl.ds(c * fc, fc)
        pltpu.make_async_copy(feats_hbm.at[0, :, cols], fbuf.at[:, cols], feat_sem.at[c]).wait()
        scaled = (gw[:, c * fc : (c + 1) * fc].astype(F32) * gain[:, c * fc : (c + 1) * fc]).astype(BF)

        def rows_body(i, _):
            rows = pl.ds(pl.multiple_of(i * 64, 64), 64)
            acc = jnp.zeros((64, 128), F32)
            for k in range(fc // 128):
                x = fbuf[rows, c * fc + k * 128 : c * fc + (k + 1) * 128].astype(F32)
                acc = acc + x * x
            ssq[rows, :] = acc if c == 0 else ssq[rows, :] + acc
            return 0

        lax.fori_loop(0, span // 64, rows_body, 0)
        prod = mm(fbuf[:, c * fc : (c + 1) * fc], scaled, NT)
        x0[...] = prod if c == 0 else x0[...] + prod

    loads["e"].wait()
    loads["h"].wait()
    loads["p0"].wait()
    loads["o0"].wait()
    fuse(0)
    loads["p1"].wait()
    loads["o1"].wait()
    fuse(1)
    loads["gain"].wait()
    loads["gw"].wait()
    feat_chunk(0)
    feat_chunk(1)
    pl.semaphore_wait(barrier, L * X + chips - 1)
    send_shares(0)
    send_shares(1)
    for c in range(2, FEAT_CHUNKS):
        feat_chunk(c)

    loads["noise"].wait()
    loads["es"].wait()
    loads["hs"].wait()
    loads["qk"].wait()
    scale = lax.rsqrt(jnp.sum(ssq[...], axis=-1, keepdims=True) * (1.0 / D) + 1e-06)
    rms[...] = jnp.broadcast_to(scale, rms.shape)
    xz = x0[...] * scale
    x0[...] = xz
    sig = jnp.full((1, chans), sigma_ref[0], F32)
    xin[...] = ((xz + sig * noise[...].T) * lax.rsqrt(sig * sig + 1.0)).astype(BF)

    def straight(n):
        e = ewin_s[n]
        if win_s != part_s:
            lane = lax.broadcasted_iota(jnp.int32, (chans, win_s), 1)
            keep = jnp.logical_and(lane >= off_s, lane < off_s + part_s)
            e = jnp.where(keep, e.astype(F32), 0.0).astype(BF)
        return mm(hwin_s[n], e, NT)

    bent = (straight(1) - straight(0)).astype(BF)
    none = jnp.zeros_like(bent)

    def packed(left, rightT):
        blank = jnp.zeros_like(rightT)
        low = mm(left[:half], jnp.concatenate([rightT, blank], axis=0), NT)
        return low + mm(left[half:], jnp.concatenate([blank, rightT], axis=0), NT)

    sum_shares(0)
    sum_shares(1)
    total = packed(xin[...], bent)

    fold = math.log2(math.e) / math.sqrt(HD)
    for n in range(2):
        drain(rx.at[n], r_ax.at[n])
        mats = [
            jnp.concatenate([wfull[n, (2 * j + h) * chans : (2 * j + h + 1) * chans] for h in range(2)], axis=1)
            for j in range(4)
        ]

        def rows_body(i, _, n=n, mats=mats):
            rows = pl.ds(pl.multiple_of(i * 128, 128), 128)
            x = xin[rows, :]
            for j in range(3):
                a = mm(x, mats[j]) * 0.5
                act = a * jnp.tanh(a) + a
                for h in range(2):
                    t = act[:, h * HD : (h + 1) * HD]
                    if j == 2:
                        vext[h, rows, 0:HD] = t.astype(BF)
                        continue
                    mean = jnp.mean(t * t, axis=-1, keepdims=True)
                    row = qk_ref[2 * n + j : 2 * n + j + 1, :]
                    if j == 0:
                        row = row * fold
                    t = (t * lax.rsqrt(mean + 1e-06) * row).astype(BF)
                    if j == 0:
                        qbuf[h, rows, :] = t
                    else:
                        kbuf[h, rows, :] = t
            return 0

        lax.fori_loop(0, span // 128, rows_body, 0)
        for b in range(span // QBLOCK):
            rows = slice(b * QBLOCK, (b + 1) * QBLOCK)
            for h in range(2):
                weights = jnp.exp2(mm(qbuf[h, rows, :], kbuf[h], NT)).astype(BF)
                both = mm(weights, vext[h])
                obuf[rows, h * HD : (h + 1) * HD] = (both[:, :HD] / both[:, HD:]).astype(BF)
        field = packed(obuf[...], mats[3])
        total = total + field if n else total - field

    tsend[...] = (total * lw_ref[0]).astype(BF)
    blocks = L * pairs // 2
    trows = half // blocks

    def block_of(peer):
        return pl.ds(pl.multiple_of((peer["seq"] // 4 * L + peer["level"]) * trows, trows), trows)

    me = {"level": l, "seq": s}
    spot_b = s // 2 * L + l
    b1[spot_b] = tsend[block_of(me), :]
    for i in range(1, chips):
        peer = chip(i)
        remote(tsend.at[block_of(peer)], b1.at[spot_b], s_b1, r_b1, peer)
    drain(b1.at[pl.ds(0, chips - 1)], r_b1)
    acc = b1[0].astype(F32)
    for i in range(1, chips):
        acc = acc + b1[i].astype(F32)
    b2[core] = acc
    remote(b2.at[core], b2.at[core], s_b2, r_b2, {"seq": mate})
    drain(b2.at[0], r_b2)
    mine_b = block_of(me)
    gfull[mine_b, :] = (b2[0] + b2[1]).astype(BF)
    near = [
        {"level": lax.rem(l + i % L, L), "seq": lax.rem(s + 4 * (i // L), S)} for i in range(1, blocks)
    ]
    for peer in near:
        remote(gfull.at[mine_b], gfull.at[mine_b], s_b3, r_b3, peer)
    drain(b1.at[pl.ds(0, blocks - 1)], r_b3)

    cut = D // X
    side = cut // 2
    lane = lax.broadcasted_iota(jnp.int32, (half, 2 * chans), 1)
    scaling = jnp.where(lane < chans, rms[0:half, :], rms[half:, :])
    turned = (gfull[...].astype(F32) * scaling).T.astype(BF)
    for o in ((2, 1, 3) if X == 4 else tuple(range(1, X))) + (0,):
        to = lax.rem(d + o, X)
        cols = pl.ds(pl.multiple_of(to * cut + core * side, 128), side)
        term = mm(turned[:chans], fbuf[0:half, cols]) + mm(turned[chans:], fbuf[half:, cols])
        if o:
            psend[o - 1] = term.astype(BF)
            remote(psend.at[o - 1], crecv.at[d], s_c, r_c, {"dp": to})
        else:
            crecv[d] = term.astype(BF)

    rows_h = span // S
    first = s * rows_h
    which = first // half
    own = pl.ds(pl.multiple_of(first, rows_h), rows_h)
    g_own = gfull[pl.ds(pl.multiple_of(first - which * half, rows_h), rows_h), :].astype(F32)
    g_own = jnp.where(which == 0, g_own, pltpu.roll(g_own, chans, 1))[:, :chans]
    inner = jnp.sum(g_own * x0[own, :], axis=-1, keepdims=True) * (1.0 / D)
    scale_own = rms[own, 0:1]
    lessen = scale_own * inner
    g_own = g_own.astype(BF)
    for c in range(FEAT_CHUNKS):
        cols = slice(c * fc, (c + 1) * fc)
        grad = mm(g_own, gw[:, cols]) * gain[:, cols] - fbuf[own, cols].astype(F32) * lessen
        oh_ref[:, cols] = (grad * scale_own).astype(BF)

    drain(crecv.at[pl.ds(0, X - 1)], r_c)
    acc = crecv[0].astype(F32)
    for i in range(1, X):
        acc = acc + crecv[i].astype(F32)
    factor = 1.0 / math.sqrt(X * span)
    mine = pl.ds(pl.multiple_of(d * cut + core * side, 128), side)
    spot = pl.ds(pl.multiple_of(core * side, 128), side)
    ow_ref[:, spot] = acc * (gain[:, mine] * factor)
    remote(ow_ref.at[:, spot], ow_ref.at[:, spot], s_k, r_k, {"seq": mate})
    drain(psend, s_c)
    for n in range(2):
        drain(rx.at[n], s_rx.at[n])
        drain(rx.at[n], s_ax.at[n])
    drain(b1.at[pl.ds(0, chips - 1)], s_b1)
    drain(b2.at[0], s_b2)
    drain(b1.at[pl.ds(0, blocks - 1)], s_b3)

    drain(ow_ref.at[:, 0:side], r_k)
    block = pl.ds(pl.multiple_of(d * cut, 128), cut)
    inside = jnp.sum(ow_ref[...] * gw[:, block].astype(F32), axis=0, keepdims=True)
    og_ref[...] = inside / gain[:, block]
    drain(ow_ref.at[:, 0:side], s_k)


def on_device(feats, gen_gain, gen_weight, noise, sigmas, level_weights, embed, proj_in, proj_out, head_out, qk_gain):
    sizes = L, S, X = tuple(lax.axis_size(a) for a in ("level", "seq", "dp"))
    span, D = feats.shape[1:]
    chans = gen_weight.shape[1]
    part = proj_in.shape[2]
    win_a = part if part % 128 == 0 else part + 64
    win_s = D // S if D // S % 128 == 0 else D // S + 64
    half = span // 2
    side = D // X // 2
    rows_h = span // S
    hbm = pl.BlockSpec(memory_space=pltpu.HBM)
    vmem = pl.BlockSpec(memory_space=pltpu.VMEM)
    smem = pl.BlockSpec(memory_space=pltpu.SMEM)
    V = pltpu.VMEM
    dma = pltpu.SemaphoreType.DMA
    scratch = [
        V((4, HD), F32),
        V((span, D), BF), V((1, D), F32), V((chans, D), BF), V((chans, span), F32),
        V((2, chans, win_a), BF), V((2, chans, win_a), BF), V((2, chans, win_s), BF), V((2, chans, win_s), BF),
        V((2, 4, win_a, 2 * HD), BF),
        V((2, 8 * chans, HD), BF), V((2, L * X - 1, 8 * chans // (L * X), HD), BF), V((2, 8 * chans, HD), BF),
        V((span, 128), F32), V((span, chans), F32), V((span, 128), F32), V((span, chans), BF),
        V((2, span, HD), BF), V((2, span, HD), BF), V((2, span, 2 * HD), BF), V((span, 2 * HD), BF),
        V((half, 2 * chans), BF), V((L * S // 2, 4 * half // (L * S), 2 * chans), BF),
        V((2, 4 * half // (L * S), 2 * chans), F32),
        V((half, 2 * chans), BF), V((X - 1, chans, side), BF), V((X, chans, side), BF),
        dma((12,)), dma((FEAT_CHUNKS,)),
    ] + [dma((2,))] * 4 + [dma] * 10
    out_h, out_w, out_g = pl.pallas_call(
        functools.partial(kernel, sizes),
        out_shape=(
            V((rows_h, D), BF),
            V((chans, 2 * side), F32),
            V((1, 2 * side), F32),
        ),
        in_specs=[smem] * 2 + [hbm] * 9,
        out_specs=(vmem, vmem, vmem),
        scratch_shapes=scratch,
        compiler_params=pltpu.CompilerParams(
            collective_id=0, has_side_effects=True, vmem_limit_bytes=40 * 1024 * 1024
        ),
    )(
        sigmas,
        level_weights,
        *(
            pltpu.with_memory_space_constraint(a, pltpu.HBM)
            for a in (
                qk_gain.reshape(4, HD), feats, gen_gain[None], gen_weight.T, noise[0, 0].T,
                embed, proj_in, jnp.swapaxes(proj_out, 1, 2), jnp.swapaxes(head_out, 1, 2),
            )
        ),
    )
    return out_h[None], out_w.T, out_g[0]


def solution(mesh):
    in_specs = (
        P("dp", None, None),
        P(),
        P(),
        P("level", "dp", None, None),
        P("level"),
        P("level"),
        P(),
        P(None, None, ("level", "dp"), "seq"),
        P(None, "seq", ("level", "dp")),
        P(),
        P(),
    )
    out_specs = (P("dp", "seq", None), P("dp", None), P("dp"))
    return jax.shard_map(on_device, mesh=mesh, in_specs=in_specs, out_specs=out_specs, check_vma=False)
```

```python
import functools
import math

import jax
import jax.numpy as jnp
from jax import lax
from jax.experimental import pallas as pl
from jax.experimental.pallas import tpu as pltpu
from jax.sharding import PartitionSpec as P

HD = 128
BF = jnp.bfloat16
F32 = jnp.float32
MESH = pl.DeviceIdType.MESH
NT = (((1,), (1,)), ((), ()))
NN = (((1,), (0,)), ((), ()))
FEAT_CHUNKS = 5
QBLOCK = 256


def mm(a, b, dims=NN):
    return lax.dot_general(a, b, dims, preferred_element_type=F32)


def window(index, part):
    if part % 128 == 0:
        return index * part, part, 0
    assert part % 128 == 64
    offset = lax.rem(index, 2) * 64
    return index * part - offset, part + 64, offset


def kernel(
    sizes,
    sigma_ref, lw_ref, qk_hbm, feats_hbm, gain_hbm, gw_hbm, noise_hbm, embed_hbm, pin_hbm, po_hbm, ho_hbm,
    oh_ref, ow_ref, og_ref,
    qk_ref, fbuf, gain, gw, noise, ewin, hwin, ewin_s, hwin_s, wbuf,
    wpart, rx, wfull,
    ssq, x0, rms, xin, qbuf, kbuf, vext, obuf,
    tsend, b1, b2, gfull, psend, crecv,
    in_sem, feat_sem,
    s_rx, r_rx, s_ax, r_ax,
    s_b1, r_b1, s_b2, r_b2, s_b3, r_b3, s_c, r_c, s_k, r_k,
):
    L, S, X = sizes
    D = fbuf.shape[1]
    span = fbuf.shape[0]
    chans = gw.shape[0]
    half = span // 2
    l, s, d = lax.axis_index("level"), lax.axis_index("seq"), lax.axis_index("dp")
    core = lax.rem(s, 2)
    mate = s + 1 - 2 * core

    mirror = [l, l + 1 - 2 * lax.rem(l, 2), l + 2 - 4 * (l // 2), L - 1 - l]
    team = [
        {"level": mirror[a], "dp": lax.rem(d + b, X)} for a in (3, 2, 1, 0) for b in (2, 1, 3, 0) if a or b
    ]
    Z, Y = 2 * L, S // 4
    chips = Z * Y
    y, z = s // 4, lax.rem(s // 2, 2) * L + l

    def chip(step_y, step_z):
        to_y, to_z = lax.rem(y + step_y, Y), lax.rem(z + step_z, Z)
        return {"level": lax.rem(to_z, L), "seq": 4 * to_y + 2 * (to_z // L) + core}

    def around(steps_z):
        steps = [(a, b) for a in range(Y) for b in steps_z if a or b]
        far = lambda step: min(step[0], Y - step[0]) + min(step[1], Z - step[1])
        return [chip(*step) for step in sorted(steps, key=far, reverse=True)]

    others = around(range(Z))

    def remote(src, dst, ssem, rsem, where):
        copy = pltpu.make_async_remote_copy(
            src_ref=src, dst_ref=dst, send_sem=ssem, recv_sem=rsem, device_id=where, device_id_type=MESH
        )
        copy.start()
        return copy

    def drain(ref, sem):
        pltpu.make_async_copy(ref, ref, sem).wait()

    barrier = pltpu.get_barrier_semaphore()
    for peer in others + team + [{"seq": mate}]:
        pl.semaphore_signal(barrier, inc=1, device_id=peer, device_id_type=MESH)

    part = pin_hbm.shape[2]
    start_a, win_a, off_a = window(l * X + d, part)
    part_s = D // S
    start_s, win_s, off_s = window(s, part_s)
    if win_a != part:
        start_a = pl.multiple_of(start_a, 128)
        off_a = pl.multiple_of(off_a, 64)
    if win_s != part_s:
        start_s = pl.multiple_of(start_s, 128)
    cols_a, cols_s = pl.ds(start_a, win_a), pl.ds(start_s, win_s)
    inner_rows = pl.ds(off_a, part)

    loads = {}

    def load(name, src, dst):
        k = len(loads)
        copy = pltpu.make_async_copy(src, dst, in_sem.at[k])
        copy.start()
        loads[name] = copy

    load("e", embed_hbm.at[:, :, cols_a], ewin)
    load("p0", pin_hbm.at[0], wbuf.at[0, pl.ds(0, 3), inner_rows])
    load("h", ho_hbm.at[:, :, cols_a], hwin)
    load("o0", po_hbm.at[0], wbuf.at[0, 3, inner_rows])
    load("p1", pin_hbm.at[1], wbuf.at[1, pl.ds(0, 3), inner_rows])
    load("o1", po_hbm.at[1], wbuf.at[1, 3, inner_rows])
    load("gain", gain_hbm, gain)
    load("gw", gw_hbm, gw)
    fc = D // FEAT_CHUNKS
    for c in range(FEAT_CHUNKS):
        pltpu.make_async_copy(
            feats_hbm.at[0, :, pl.ds(c * fc, fc)], fbuf.at[:, pl.ds(c * fc, fc)], feat_sem.at[c]
        ).start()
    load("es", embed_hbm.at[:, :, cols_s], ewin_s)
    load("hs", ho_hbm.at[:, :, cols_s], hwin_s)
    load("noise", noise_hbm, noise)
    load("qk", qk_hbm, qk_ref)

    if win_a != part:
        pad = pl.ds(pl.multiple_of((part // 64) * 64 - (part // 64) * off_a, 64), 64)
        for n in range(2):
            for j in range(4):
                wbuf[n, j, pad, :] = jnp.zeros((64, wbuf.shape[3]), BF)
    for h in range(2):
        vext[h, :, HD:] = jnp.ones((span, HD), BF)

    def fuse(n):
        for j in range(4):
            left = ewin if j < 3 else hwin
            x = mm(left[n], wbuf[n, j]).astype(BF)
            base = 2 * j * chans
            wpart[n, base : base + chans, :] = x[:, :HD]
            wpart[n, base + chans : base + 2 * chans, :] = x[:, HD:]

    share = 8 * chans // (L * X)

    def share_rows(peer):
        return pl.ds(pl.multiple_of((peer["level"] * X + peer["dp"]) * share, share), share)

    own_share = share_rows({"level": l, "dp": d})

    def send_shares(n):
        for o, peer in enumerate(team):
            remote(wpart.at[n, share_rows(peer)], rx.at[n, o], s_rx.at[n], r_rx.at[n], peer)

    def sum_shares(n):
        drain(rx.at[n], r_rx.at[n])
        total = wpart[n, own_share, :].astype(F32)
        for o in range(len(team)):
            total = total + rx[n, o].astype(F32)
        wfull[n, own_share, :] = total.astype(BF)
        for peer in team:
            remote(wfull.at[n, own_share], wfull.at[n, own_share], s_ax.at[n], r_ax.at[n], peer)

    def feat_chunk(c):
        cols = pl.ds(c * fc, fc)
        pltpu.make_async_copy(feats_hbm.at[0, :, cols], fbuf.at[:, cols], feat_sem.at[c]).wait()
        scaled = (gw[:, c * fc : (c + 1) * fc].astype(F32) * gain[:, c * fc : (c + 1) * fc]).astype(BF)

        def rows_body(i, _):
            rows = pl.ds(pl.multiple_of(i * 64, 64), 64)
            acc = jnp.zeros((64, 128), F32)
            for k in range(fc // 128):
                x = fbuf[rows, c * fc + k * 128 : c * fc + (k + 1) * 128].astype(F32)
                acc = acc + x * x
            ssq[rows, :] = acc if c == 0 else ssq[rows, :] + acc
            return 0

        lax.fori_loop(0, span // 64, rows_body, 0)
        prod = mm(fbuf[:, c * fc : (c + 1) * fc], scaled, NT)
        x0[...] = prod if c == 0 else x0[...] + prod

    loads["e"].wait()
    loads["h"].wait()
    loads["p0"].wait()
    loads["o0"].wait()
    fuse(0)
    loads["p1"].wait()
    loads["o1"].wait()
    fuse(1)
    loads["gain"].wait()
    loads["gw"].wait()
    feat_chunk(0)
    feat_chunk(1)
    pl.semaphore_wait(barrier, L * X + chips - 1)
    send_shares(0)
    send_shares(1)
    for c in range(2, FEAT_CHUNKS):
        feat_chunk(c)

    loads["noise"].wait()
    loads["es"].wait()
    loads["hs"].wait()
    loads["qk"].wait()
    scale = lax.rsqrt(jnp.sum(ssq[...], axis=-1, keepdims=True) * (1.0 / D) + 1e-06)
    rms[...] = jnp.broadcast_to(scale, rms.shape)
    xz = x0[...] * scale
    x0[...] = xz
    sig = jnp.full((1, chans), sigma_ref[0], F32)
    xin[...] = ((xz + sig * noise[...].T) * lax.rsqrt(sig * sig + 1.0)).astype(BF)

    def straight(n):
        e = ewin_s[n]
        if win_s != part_s:
            lane = lax.broadcasted_iota(jnp.int32, (chans, win_s), 1)
            keep = jnp.logical_and(lane >= off_s, lane < off_s + part_s)
            e = jnp.where(keep, e.astype(F32), 0.0).astype(BF)
        return mm(hwin_s[n], e, NT)

    bent = (straight(1) - straight(0)).astype(BF)
    none = jnp.zeros_like(bent)

    def packed(left, rightT):
        blank = jnp.zeros_like(rightT)
        low = mm(left[:half], jnp.concatenate([rightT, blank], axis=0), NT)
        return low + mm(left[half:], jnp.concatenate([blank, rightT], axis=0), NT)

    sum_shares(0)
    sum_shares(1)
    total = packed(xin[...], bent)

    fold = math.log2(math.e) / math.sqrt(HD)
    for n in range(2):
        drain(rx.at[n], r_ax.at[n])
        mats = [
            jnp.concatenate([wfull[n, (2 * j + h) * chans : (2 * j + h + 1) * chans] for h in range(2)], axis=1)
            for j in range(4)
        ]

        def rows_body(i, _, n=n, mats=mats):
            rows = pl.ds(pl.multiple_of(i * 128, 128), 128)
            x = xin[rows, :]
            for j in range(3):
                a = mm(x, mats[j]) * 0.5
                act = a * jnp.tanh(a) + a
                for h in range(2):
                    t = act[:, h * HD : (h + 1) * HD]
                    if j == 2:
                        vext[h, rows, 0:HD] = t.astype(BF)
                        continue
                    mean = jnp.mean(t * t, axis=-1, keepdims=True)
                    row = qk_ref[2 * n + j : 2 * n + j + 1, :]
                    if j == 0:
                        row = row * fold
                    t = (t * lax.rsqrt(mean + 1e-06) * row).astype(BF)
                    if j == 0:
                        qbuf[h, rows, :] = t
                    else:
                        kbuf[h, rows, :] = t
            return 0

        lax.fori_loop(0, span // 128, rows_body, 0, unroll=True)
        for b in range(span // QBLOCK):
            rows = slice(b * QBLOCK, (b + 1) * QBLOCK)
            for h in range(2):
                weights = jnp.exp2(mm(qbuf[h, rows, :], kbuf[h], NT)).astype(BF)
                both = mm(weights, vext[h])
                obuf[rows, h * HD : (h + 1) * HD] = (both[:, :HD] / both[:, HD:]).astype(BF)
        field = packed(obuf[...], mats[3])
        total = total + field if n else total - field

    tsend[...] = (total * lw_ref[0]).astype(BF)
    blocks = chips // 2
    trows = half // blocks

    def block_of(peer):
        return pl.ds(pl.multiple_of((peer["seq"] // 4 * L + peer["level"]) * trows, trows), trows)

    me = {"level": l, "seq": s}
    spot_b = s // 2 * L + l
    b1[spot_b] = tsend[block_of(me), :]
    for peer in others:
        remote(tsend.at[block_of(peer)], b1.at[spot_b], s_b1, r_b1, peer)
    drain(b1.at[pl.ds(0, chips - 1)], r_b1)
    acc = b1[0].astype(F32)
    for i in range(1, chips):
        acc = acc + b1[i].astype(F32)
    b2[core] = acc
    remote(b2.at[core], b2.at[core], s_b2, r_b2, {"seq": mate})
    drain(b2.at[0], r_b2)
    mine_b = block_of(me)
    gfull[mine_b, :] = (b2[0] + b2[1]).astype(BF)
    for peer in around((0, 1, 2, Z - 1)):
        remote(gfull.at[mine_b], gfull.at[mine_b], s_b3, r_b3, peer)
    drain(b1.at[pl.ds(0, blocks - 1)], r_b3)

    cut = D // X
    side = cut // 2
    lane = lax.broadcasted_iota(jnp.int32, (half, 2 * chans), 1)
    scaling = jnp.where(lane < chans, rms[0:half, :], rms[half:, :])
    turned = (gfull[...].astype(F32) * scaling).T.astype(BF)
    for o in ((2, 1, 3) if X == 4 else tuple(range(1, X))) + (0,):
        to = lax.rem(d + o, X)
        cols = pl.ds(pl.multiple_of(to * cut + core * side, 128), side)
        term = mm(turned[:chans], fbuf[0:half, cols]) + mm(turned[chans:], fbuf[half:, cols])
        if o:
            psend[o - 1] = term.astype(BF)
            remote(psend.at[o - 1], crecv.at[d], s_c, r_c, {"dp": to})
        else:
            crecv[d] = term.astype(BF)

    rows_h = span // S
    first = s * rows_h
    which = first // half
    own = pl.ds(pl.multiple_of(first, rows_h), rows_h)
    g_own = gfull[pl.ds(pl.multiple_of(first - which * half, rows_h), rows_h), :].astype(F32)
    g_own = jnp.where(which == 0, g_own, pltpu.roll(g_own, chans, 1))[:, :chans]
    inner = jnp.sum(g_own * x0[own, :], axis=-1, keepdims=True) * (1.0 / D)
    scale_own = rms[own, 0:1]
    lessen = scale_own * inner
    g_own = g_own.astype(BF)
    for c in range(FEAT_CHUNKS):
        cols = slice(c * fc, (c + 1) * fc)
        grad = mm(g_own, gw[:, cols]) * gain[:, cols] - fbuf[own, cols].astype(F32) * lessen
        oh_ref[:, cols] = (grad * scale_own).astype(BF)

    drain(crecv.at[pl.ds(0, X - 1)], r_c)
    acc = crecv[0].astype(F32)
    for i in range(1, X):
        acc = acc + crecv[i].astype(F32)
    factor = 1.0 / math.sqrt(X * span)
    mine = pl.ds(pl.multiple_of(d * cut + core * side, 128), side)
    spot = pl.ds(pl.multiple_of(core * side, 128), side)
    ow_ref[:, spot] = acc * (gain[:, mine] * factor)
    remote(ow_ref.at[:, spot], ow_ref.at[:, spot], s_k, r_k, {"seq": mate})
    drain(psend, s_c)
    for n in range(2):
        drain(rx.at[n], s_rx.at[n])
        drain(rx.at[n], s_ax.at[n])
    drain(b1.at[pl.ds(0, chips - 1)], s_b1)
    drain(b2.at[0], s_b2)
    drain(b1.at[pl.ds(0, blocks - 1)], s_b3)

    drain(ow_ref.at[:, 0:side], r_k)
    block = pl.ds(pl.multiple_of(d * cut, 128), cut)
    inside = jnp.sum(ow_ref[...] * gw[:, block].astype(F32), axis=0, keepdims=True)
    og_ref[...] = inside / gain[:, block]
    drain(ow_ref.at[:, 0:side], s_k)


def on_device(feats, gen_gain, gen_weight, noise, sigmas, level_weights, embed, proj_in, proj_out, head_out, qk_gain):
    sizes = L, S, X = tuple(lax.axis_size(a) for a in ("level", "seq", "dp"))
    span, D = feats.shape[1:]
    chans = gen_weight.shape[1]
    part = proj_in.shape[2]
    win_a = part if part % 128 == 0 else part + 64
    win_s = D // S if D // S % 128 == 0 else D // S + 64
    half = span // 2
    side = D // X // 2
    rows_h = span // S
    hbm = pl.BlockSpec(memory_space=pltpu.HBM)
    vmem = pl.BlockSpec(memory_space=pltpu.VMEM)
    smem = pl.BlockSpec(memory_space=pltpu.SMEM)
    V = pltpu.VMEM
    dma = pltpu.SemaphoreType.DMA
    scratch = [
        V((4, HD), F32),
        V((span, D), BF), V((1, D), F32), V((chans, D), BF), V((chans, span), F32),
        V((2, chans, win_a), BF), V((2, chans, win_a), BF), V((2, chans, win_s), BF), V((2, chans, win_s), BF),
        V((2, 4, win_a, 2 * HD), BF),
        V((2, 8 * chans, HD), BF), V((2, L * X - 1, 8 * chans // (L * X), HD), BF), V((2, 8 * chans, HD), BF),
        V((span, 128), F32), V((span, chans), F32), V((span, 128), F32), V((span, chans), BF),
        V((2, span, HD), BF), V((2, span, HD), BF), V((2, span, 2 * HD), BF), V((span, 2 * HD), BF),
        V((half, 2 * chans), BF), V((L * S // 2, 4 * half // (L * S), 2 * chans), BF),
        V((2, 4 * half // (L * S), 2 * chans), F32),
        V((half, 2 * chans), BF), V((X - 1, chans, side), BF), V((X, chans, side), BF),
        dma((12,)), dma((FEAT_CHUNKS,)),
    ] + [dma((2,))] * 4 + [dma] * 10
    out_h, out_w, out_g = pl.pallas_call(
        functools.partial(kernel, sizes),
        out_shape=(
            V((rows_h, D), BF),
            V((chans, 2 * side), F32),
            V((1, 2 * side), F32),
        ),
        in_specs=[smem] * 2 + [hbm] * 9,
        out_specs=(vmem, vmem, vmem),
        scratch_shapes=scratch,
        compiler_params=pltpu.CompilerParams(
            collective_id=0, has_side_effects=True, vmem_limit_bytes=40 * 1024 * 1024
        ),
    )(
        sigmas,
        level_weights,
        *(
            pltpu.with_memory_space_constraint(a, pltpu.HBM)
            for a in (
                qk_gain.reshape(4, HD), feats, gen_gain[None], gen_weight.T, noise[0, 0].T,
                embed, proj_in, jnp.swapaxes(proj_out, 1, 2), jnp.swapaxes(head_out, 1, 2),
            )
        ),
    )
    return out_h[None], out_w.T, out_g[0]


def solution(mesh):
    in_specs = (
        P("dp", None, None),
        P(),
        P(),
        P("level", "dp", None, None),
        P("level"),
        P("level"),
        P(),
        P(None, None, ("level", "dp"), "seq"),
        P(None, "seq", ("level", "dp")),
        P(),
        P(),
    )
    out_specs = (P("dp", "seq", None), P("dp", None), P("dp"))
    return jax.shard_map(on_device, mesh=mesh, in_specs=in_specs, out_specs=out_specs, check_vma=False)
```

```python
import functools
import math

import jax
import jax.numpy as jnp
from jax import lax
from jax.experimental import pallas as pl
from jax.experimental.pallas import tpu as pltpu
from jax.sharding import PartitionSpec as P

HD = 128
BF = jnp.bfloat16
F32 = jnp.float32
MESH = pl.DeviceIdType.MESH
NT = (((1,), (1,)), ((), ()))
NN = (((1,), (0,)), ((), ()))
FEAT_CHUNKS = 5
QBLOCK = 256


def mm(a, b, dims=NN):
    return lax.dot_general(a, b, dims, preferred_element_type=F32)


def window(index, part):
    if part % 128 == 0:
        return index * part, part, 0
    assert part % 128 == 64
    offset = lax.rem(index, 2) * 64
    return index * part - offset, part + 64, offset


def kernel(
    sizes,
    sigma_ref, lw_ref, qk_hbm, feats_hbm, gain_hbm, gw_hbm, noise_hbm, embed_hbm, pin_hbm, po_hbm, ho_hbm,
    oh_ref, ow_ref, og_ref,
    qk_ref, fbuf, gain, gw, noise, ewin, hwin, ewin_s, hwin_s, wbuf,
    wpart, rx, wfull,
    ssq, x0, rms, xin, qbuf, kbuf, vext, obuf,
    tsend, b1, gfull, psend, crecv,
    in_sem, feat_sem,
    s_rx, r_rx, s_ax, r_ax,
    s_b1, r_b1, s_b3, r_b3, s_c, r_c, s_k, r_k,
):
    L, S, X = sizes
    D = fbuf.shape[1]
    span = fbuf.shape[0]
    chans = gw.shape[0]
    half = span // 2
    l, s, d = lax.axis_index("level"), lax.axis_index("seq"), lax.axis_index("dp")
    core = lax.rem(s, 2)
    mate = s + 1 - 2 * core

    mirror = [l, l + 1 - 2 * lax.rem(l, 2), l + 2 - 4 * (l // 2), L - 1 - l]
    team = [
        {"level": mirror[a], "dp": lax.rem(d + b, X)} for a in (3, 2, 1, 0) for b in (2, 1, 3, 0) if a or b
    ]
    Z, Y = 2 * L, S // 4
    chips = Z * Y
    y, z = s // 4, lax.rem(s // 2, 2) * L + l

    def steps(steps_z):
        far = lambda step: min(step[0], Y - step[0]) + min(step[1], Z - step[1])
        return sorted([(a, b) for a in range(Y) for b in steps_z if a or b], key=far, reverse=True)

    def chip(step):
        to_y, to_z = lax.rem(y + step[0], Y), lax.rem(z + step[1], Z)
        return lax.rem(to_z, L), 4 * to_y + 2 * (to_z // L), to_z // L

    def on_chip(step, of_core):
        to_level, to_seq, z_hi = chip(step)
        return {"level": to_level, "seq": to_seq + (z_hi if of_core is None else of_core)}

    def remote(src, dst, ssem, rsem, where):
        copy = pltpu.make_async_remote_copy(
            src_ref=src, dst_ref=dst, send_sem=ssem, recv_sem=rsem, device_id=where, device_id_type=MESH
        )
        copy.start()
        return copy

    def drain(ref, sem):
        pltpu.make_async_copy(ref, ref, sem).wait()

    barrier = pltpu.get_barrier_semaphore()
    for peer in [on_chip(step, c) for step in steps(range(Z)) for c in range(2)] + team + [{"seq": mate}]:
        pl.semaphore_signal(barrier, inc=1, device_id=peer, device_id_type=MESH)

    part = pin_hbm.shape[2]
    start_a, win_a, off_a = window(l * X + d, part)
    part_s = D // S
    start_s, win_s, off_s = window(s, part_s)
    if win_a != part:
        start_a = pl.multiple_of(start_a, 128)
        off_a = pl.multiple_of(off_a, 64)
    if win_s != part_s:
        start_s = pl.multiple_of(start_s, 128)
    cols_a, cols_s = pl.ds(start_a, win_a), pl.ds(start_s, win_s)
    inner_rows = pl.ds(off_a, part)

    loads = {}

    def load(name, src, dst):
        k = len(loads)
        copy = pltpu.make_async_copy(src, dst, in_sem.at[k])
        copy.start()
        loads[name] = copy

    load("e", embed_hbm.at[:, :, cols_a], ewin)
    load("p0", pin_hbm.at[0], wbuf.at[0, pl.ds(0, 3), inner_rows])
    load("h", ho_hbm.at[:, :, cols_a], hwin)
    load("o0", po_hbm.at[0], wbuf.at[0, 3, inner_rows])
    load("p1", pin_hbm.at[1], wbuf.at[1, pl.ds(0, 3), inner_rows])
    load("o1", po_hbm.at[1], wbuf.at[1, 3, inner_rows])
    load("gain", gain_hbm, gain)
    load("gw", gw_hbm, gw)
    fc = D // FEAT_CHUNKS
    for c in range(FEAT_CHUNKS):
        pltpu.make_async_copy(
            feats_hbm.at[0, :, pl.ds(c * fc, fc)], fbuf.at[:, pl.ds(c * fc, fc)], feat_sem.at[c]
        ).start()
    load("es", embed_hbm.at[:, :, cols_s], ewin_s)
    load("hs", ho_hbm.at[:, :, cols_s], hwin_s)
    load("noise", noise_hbm, noise)
    load("qk", qk_hbm, qk_ref)

    if win_a != part:
        pad = pl.ds(pl.multiple_of((part // 64) * 64 - (part // 64) * off_a, 64), 64)
        for n in range(2):
            for j in range(4):
                wbuf[n, j, pad, :] = jnp.zeros((64, wbuf.shape[3]), BF)
    for h in range(2):
        vext[h, :, HD:] = jnp.ones((span, HD), BF)

    def fuse(n):
        for j in range(4):
            left = ewin if j < 3 else hwin
            x = mm(left[n], wbuf[n, j]).astype(BF)
            base = 2 * j * chans
            wpart[n, base : base + chans, :] = x[:, :HD]
            wpart[n, base + chans : base + 2 * chans, :] = x[:, HD:]

    share = 8 * chans // (L * X)

    def share_rows(peer):
        return pl.ds(pl.multiple_of((peer["level"] * X + peer["dp"]) * share, share), share)

    own_share = share_rows({"level": l, "dp": d})

    def send_shares(n):
        for o, peer in enumerate(team):
            remote(wpart.at[n, share_rows(peer)], rx.at[n, o], s_rx.at[n], r_rx.at[n], peer)

    def sum_shares(n):
        drain(rx.at[n], r_rx.at[n])
        total = wpart[n, own_share, :].astype(F32)
        for o in range(len(team)):
            total = total + rx[n, o].astype(F32)
        wfull[n, own_share, :] = total.astype(BF)
        for peer in team:
            remote(wfull.at[n, own_share], wfull.at[n, own_share], s_ax.at[n], r_ax.at[n], peer)

    def feat_chunk(c):
        cols = pl.ds(c * fc, fc)
        pltpu.make_async_copy(feats_hbm.at[0, :, cols], fbuf.at[:, cols], feat_sem.at[c]).wait()
        scaled = (gw[:, c * fc : (c + 1) * fc].astype(F32) * gain[:, c * fc : (c + 1) * fc]).astype(BF)

        def rows_body(i, _):
            rows = pl.ds(pl.multiple_of(i * 64, 64), 64)
            acc = jnp.zeros((64, 128), F32)
            for k in range(fc // 128):
                x = fbuf[rows, c * fc + k * 128 : c * fc + (k + 1) * 128].astype(F32)
                acc = acc + x * x
            ssq[rows, :] = acc if c == 0 else ssq[rows, :] + acc
            return 0

        lax.fori_loop(0, span // 64, rows_body, 0)
        prod = mm(fbuf[:, c * fc : (c + 1) * fc], scaled, NT)
        x0[...] = prod if c == 0 else x0[...] + prod

    loads["e"].wait()
    loads["h"].wait()
    loads["p0"].wait()
    loads["o0"].wait()
    fuse(0)
    loads["p1"].wait()
    loads["o1"].wait()
    fuse(1)
    loads["gain"].wait()
    loads["gw"].wait()
    feat_chunk(0)
    feat_chunk(1)
    pl.semaphore_wait(barrier, L * X - 1 + 2 * chips - 1)
    send_shares(0)
    send_shares(1)
    for c in range(2, FEAT_CHUNKS):
        feat_chunk(c)

    loads["noise"].wait()
    loads["es"].wait()
    loads["hs"].wait()
    loads["qk"].wait()
    scale = lax.rsqrt(jnp.sum(ssq[...], axis=-1, keepdims=True) * (1.0 / D) + 1e-06)
    rms[...] = jnp.broadcast_to(scale, rms.shape)
    xz = x0[...] * scale
    x0[...] = xz
    sig = jnp.full((1, chans), sigma_ref[0], F32)
    xin[...] = ((xz + sig * noise[...].T) * lax.rsqrt(sig * sig + 1.0)).astype(BF)

    def straight(n):
        e = ewin_s[n]
        if win_s != part_s:
            lane = lax.broadcasted_iota(jnp.int32, (chans, win_s), 1)
            keep = jnp.logical_and(lane >= off_s, lane < off_s + part_s)
            e = jnp.where(keep, e.astype(F32), 0.0).astype(BF)
        return mm(hwin_s[n], e, NT)

    bent = (straight(1) - straight(0)).astype(BF)
    none = jnp.zeros_like(bent)

    def packed(left, rightT):
        blank = jnp.zeros_like(rightT)
        low = mm(left[:half], jnp.concatenate([rightT, blank], axis=0), NT)
        return low + mm(left[half:], jnp.concatenate([blank, rightT], axis=0), NT)

    sum_shares(0)
    sum_shares(1)
    total = packed(xin[...], bent)

    fold = math.log2(math.e) / math.sqrt(HD)
    for n in range(2):
        drain(rx.at[n], r_ax.at[n])
        mats = [
            jnp.concatenate([wfull[n, (2 * j + h) * chans : (2 * j + h + 1) * chans] for h in range(2)], axis=1)
            for j in range(4)
        ]

        def rows_body(i, _, n=n, mats=mats):
            rows = pl.ds(pl.multiple_of(i * 128, 128), 128)
            x = xin[rows, :]
            for j in range(3):
                a = mm(x, mats[j]) * 0.5
                act = a * jnp.tanh(a) + a
                for h in range(2):
                    t = act[:, h * HD : (h + 1) * HD]
                    if j == 2:
                        vext[h, rows, 0:HD] = t.astype(BF)
                        continue
                    mean = jnp.mean(t * t, axis=-1, keepdims=True)
                    row = qk_ref[2 * n + j : 2 * n + j + 1, :]
                    if j == 0:
                        row = row * fold
                    t = (t * lax.rsqrt(mean + 1e-06) * row).astype(BF)
                    if j == 0:
                        qbuf[h, rows, :] = t
                    else:
                        kbuf[h, rows, :] = t
            return 0

        lax.fori_loop(0, span // 128, rows_body, 0, unroll=True)
        for b in range(span // QBLOCK):
            rows = slice(b * QBLOCK, (b + 1) * QBLOCK)
            for h in range(2):
                weights = jnp.exp2(mm(qbuf[h, rows, :], kbuf[h], NT)).astype(BF)
                both = mm(weights, vext[h])
                obuf[rows, h * HD : (h + 1) * HD] = (both[:, :HD] / both[:, HD:]).astype(BF)
        field = packed(obuf[...], mats[3])
        total = total + field if n else total - field

    tsend[...] = (total * lw_ref[0]).astype(BF)
    blocks = chips // 2
    trows = half // blocks

    def block_of(peer):
        return pl.ds(pl.multiple_of((peer["seq"] // 4 * L + peer["level"]) * trows, trows), trows)

    mine_b = block_of({"level": l, "seq": s})
    owner = core == z // L
    spot_b = 2 * (s // 2 * L + l) + core
    for step in steps(range(Z)):
        peer = on_chip(step, None)
        remote(tsend.at[block_of(peer)], b1.at[spot_b], s_b1, r_b1, peer)

    @pl.when(owner)
    def _():
        b1[spot_b] = tsend[mine_b, :]
        drain(b1.at[pl.ds(0, 2 * chips - 1)], r_b1)
        acc = b1[0].astype(F32)
        for i in range(1, 2 * chips):
            acc = acc + b1[i].astype(F32)
        gfull[mine_b, :] = acc.astype(BF)
        for peer in [on_chip(step, c) for step in steps((0, 1, 2, Z - 1)) for c in range(2)] + [{"seq": mate}]:
            remote(gfull.at[mine_b], gfull.at[mine_b], s_b3, r_b3, peer)
        drain(b1.at[pl.ds(0, blocks - 1)], r_b3)

    @pl.when(jnp.logical_not(owner))
    def _():
        remote(tsend.at[mine_b], b1.at[spot_b], s_b1, r_b1, {"seq": mate})
        drain(b1.at[pl.ds(0, blocks)], r_b3)

    cut = D // X
    side = cut // 2
    lane = lax.broadcasted_iota(jnp.int32, (half, 2 * chans), 1)
    scaling = jnp.where(lane < chans, rms[0:half, :], rms[half:, :])
    turned = (gfull[...].astype(F32) * scaling).T.astype(BF)
    for o in ((2, 1, 3) if X == 4 else tuple(range(1, X))) + (0,):
        to = lax.rem(d + o, X)
        cols = pl.ds(pl.multiple_of(to * cut + core * side, 128), side)
        term = mm(turned[:chans], fbuf[0:half, cols]) + mm(turned[chans:], fbuf[half:, cols])
        if o:
            psend[o - 1] = term.astype(BF)
            remote(psend.at[o - 1], crecv.at[d], s_c, r_c, {"dp": to})
        else:
            crecv[d] = term.astype(BF)

    rows_h = span // S
    first = s * rows_h
    which = first // half
    own = pl.ds(pl.multiple_of(first, rows_h), rows_h)
    g_own = gfull[pl.ds(pl.multiple_of(first - which * half, rows_h), rows_h), :].astype(F32)
    g_own = jnp.where(which == 0, g_own, pltpu.roll(g_own, chans, 1))[:, :chans]
    inner = jnp.sum(g_own * x0[own, :], axis=-1, keepdims=True) * (1.0 / D)
    scale_own = rms[own, 0:1]
    lessen = scale_own * inner
    g_own = g_own.astype(BF)
    for c in range(FEAT_CHUNKS):
        cols = slice(c * fc, (c + 1) * fc)
        grad = mm(g_own, gw[:, cols]) * gain[:, cols] - fbuf[own, cols].astype(F32) * lessen
        oh_ref[:, cols] = (grad * scale_own).astype(BF)

    drain(crecv.at[pl.ds(0, X - 1)], r_c)
    acc = crecv[0].astype(F32)
    for i in range(1, X):
        acc = acc + crecv[i].astype(F32)
    factor = 1.0 / math.sqrt(X * span)
    mine = pl.ds(pl.multiple_of(d * cut + core * side, 128), side)
    spot = pl.ds(pl.multiple_of(core * side, 128), side)
    ow_ref[:, spot] = acc * (gain[:, mine] * factor)
    remote(ow_ref.at[:, spot], ow_ref.at[:, spot], s_k, r_k, {"seq": mate})
    drain(psend, s_c)
    for n in range(2):
        drain(rx.at[n], s_rx.at[n])
        drain(rx.at[n], s_ax.at[n])
    drain(b1.at[pl.ds(0, chips - 1)], s_b1)

    @pl.when(owner)
    def _():
        drain(b1.at[pl.ds(0, 2 * blocks - 1)], s_b3)

    @pl.when(jnp.logical_not(owner))
    def _():
        drain(b1.at[0], s_b1)


    drain(ow_ref.at[:, 0:side], r_k)
    block = pl.ds(pl.multiple_of(d * cut, 128), cut)
    inside = jnp.sum(ow_ref[...] * gw[:, block].astype(F32), axis=0, keepdims=True)
    og_ref[...] = inside / gain[:, block]
    drain(ow_ref.at[:, 0:side], s_k)


def on_device(feats, gen_gain, gen_weight, noise, sigmas, level_weights, embed, proj_in, proj_out, head_out, qk_gain):
    sizes = L, S, X = tuple(lax.axis_size(a) for a in ("level", "seq", "dp"))
    span, D = feats.shape[1:]
    chans = gen_weight.shape[1]
    part = proj_in.shape[2]
    win_a = part if part % 128 == 0 else part + 64
    win_s = D // S if D // S % 128 == 0 else D // S + 64
    half = span // 2
    side = D // X // 2
    rows_h = span // S
    hbm = pl.BlockSpec(memory_space=pltpu.HBM)
    vmem = pl.BlockSpec(memory_space=pltpu.VMEM)
    smem = pl.BlockSpec(memory_space=pltpu.SMEM)
    V = pltpu.VMEM
    dma = pltpu.SemaphoreType.DMA
    scratch = [
        V((4, HD), F32),
        V((span, D), BF), V((1, D), F32), V((chans, D), BF), V((chans, span), F32),
        V((2, chans, win_a), BF), V((2, chans, win_a), BF), V((2, chans, win_s), BF), V((2, chans, win_s), BF),
        V((2, 4, win_a, 2 * HD), BF),
        V((2, 8 * chans, HD), BF), V((2, L * X - 1, 8 * chans // (L * X), HD), BF), V((2, 8 * chans, HD), BF),
        V((span, 128), F32), V((span, chans), F32), V((span, 128), F32), V((span, chans), BF),
        V((2, span, HD), BF), V((2, span, HD), BF), V((2, span, 2 * HD), BF), V((span, 2 * HD), BF),
        V((half, 2 * chans), BF), V((L * S, 4 * half // (L * S), 2 * chans), BF),
        V((half, 2 * chans), BF), V((X - 1, chans, side), BF), V((X, chans, side), BF),
        dma((12,)), dma((FEAT_CHUNKS,)),
    ] + [dma((2,))] * 4 + [dma] * 8
    out_h, out_w, out_g = pl.pallas_call(
        functools.partial(kernel, sizes),
        out_shape=(
            V((rows_h, D), BF),
            V((chans, 2 * side), F32),
            V((1, 2 * side), F32),
        ),
        in_specs=[smem] * 2 + [hbm] * 9,
        out_specs=(vmem, vmem, vmem),
        scratch_shapes=scratch,
        compiler_params=pltpu.CompilerParams(
            collective_id=0, has_side_effects=True, vmem_limit_bytes=40 * 1024 * 1024
        ),
    )(
        sigmas,
        level_weights,
        *(
            pltpu.with_memory_space_constraint(a, pltpu.HBM)
            for a in (
                qk_gain.reshape(4, HD), feats, gen_gain[None], gen_weight.T, noise[0, 0].T,
                embed, proj_in, jnp.swapaxes(proj_out, 1, 2), jnp.swapaxes(head_out, 1, 2),
            )
        ),
    )
    return out_h[None], out_w.T, out_g[0]


def solution(mesh):
    in_specs = (
        P("dp", None, None),
        P(),
        P(),
        P("level", "dp", None, None),
        P("level"),
        P("level"),
        P(),
        P(None, None, ("level", "dp"), "seq"),
        P(None, "seq", ("level", "dp")),
        P(),
        P(),
    )
    out_specs = (P("dp", "seq", None), P("dp", None), P("dp"))
    return jax.shard_map(on_device, mesh=mesh, in_specs=in_specs, out_specs=out_specs, check_vma=False)
```

```python
import functools
import math

import jax
import jax.numpy as jnp
from jax import lax
from jax.experimental import pallas as pl
from jax.experimental.pallas import tpu as pltpu
from jax.sharding import PartitionSpec as P

HD = 128
BF = jnp.bfloat16
F32 = jnp.float32
MESH = pl.DeviceIdType.MESH
NT = (((1,), (1,)), ((), ()))
NN = (((1,), (0,)), ((), ()))
FEAT_CHUNKS = 5
QBLOCK = 256


def mm(a, b, dims=NN):
    return lax.dot_general(a, b, dims, preferred_element_type=F32)


def window(index, part):
    if part % 128 == 0:
        return index * part, part, 0
    assert part % 128 == 64
    offset = lax.rem(index, 2) * 64
    return index * part - offset, part + 64, offset


def kernel(
    sizes,
    sigma_ref, lw_ref, qk_hbm, feats_hbm, gain_hbm, gw_hbm, noise_hbm, embed_hbm, pin_hbm, po_hbm, ho_hbm,
    oh_ref, ow_ref, og_ref,
    qk_ref, fbuf, gain, gw, noise, ewin, hwin, ewin_s, hwin_s, wbuf,
    wpart, rx, wfull,
    ssq, x0, rms, xin, qbuf, kbuf, pbuf, vext, obuf,
    tsend, b1, gfull, psend, crecv,
    in_sem, feat_sem,
    s_rx, r_rx, s_ax, r_ax,
    s_b1, r_b1, s_b3, r_b3, s_c, r_c, s_k, r_k,
):
    L, S, X = sizes
    D = fbuf.shape[1]
    span = fbuf.shape[0]
    chans = gw.shape[0]
    half = span // 2
    l, s, d = lax.axis_index("level"), lax.axis_index("seq"), lax.axis_index("dp")
    core = lax.rem(s, 2)
    mate = s + 1 - 2 * core

    mirror = [l, l + 1 - 2 * lax.rem(l, 2), l + 2 - 4 * (l // 2), L - 1 - l]
    team = [
        {"level": mirror[a], "dp": lax.rem(d + b, X)} for a in (3, 2, 1, 0) for b in (2, 1, 3, 0) if a or b
    ]
    Z, Y = 2 * L, S // 4
    chips = Z * Y
    y, z = s // 4, lax.rem(s // 2, 2) * L + l

    def steps(steps_z):
        far = lambda step: min(step[0], Y - step[0]) + min(step[1], Z - step[1])
        return sorted([(a, b) for a in range(Y) for b in steps_z if a or b], key=far, reverse=True)

    def chip(step):
        to_y, to_z = lax.rem(y + step[0], Y), lax.rem(z + step[1], Z)
        return lax.rem(to_z, L), 4 * to_y + 2 * (to_z // L), to_z // L

    def on_chip(step, of_core):
        to_level, to_seq, z_hi = chip(step)
        return {"level": to_level, "seq": to_seq + (z_hi if of_core is None else of_core)}

    def remote(src, dst, ssem, rsem, where):
        copy = pltpu.make_async_remote_copy(
            src_ref=src, dst_ref=dst, send_sem=ssem, recv_sem=rsem, device_id=where, device_id_type=MESH
        )
        copy.start()
        return copy

    def drain(ref, sem):
        pltpu.make_async_copy(ref, ref, sem).wait()

    barrier = pltpu.get_barrier_semaphore()
    for peer in [on_chip(step, c) for step in steps(range(Z)) for c in range(2)] + team + [{"seq": mate}]:
        pl.semaphore_signal(barrier, inc=1, device_id=peer, device_id_type=MESH)

    part = pin_hbm.shape[2]
    start_a, win_a, off_a = window(l * X + d, part)
    part_s = D // S
    start_s, win_s, off_s = window(s, part_s)
    if win_a != part:
        start_a = pl.multiple_of(start_a, 128)
        off_a = pl.multiple_of(off_a, 64)
    if win_s != part_s:
        start_s = pl.multiple_of(start_s, 128)
    cols_a, cols_s = pl.ds(start_a, win_a), pl.ds(start_s, win_s)
    inner_rows = pl.ds(off_a, part)

    loads = {}

    def load(name, src, dst):
        k = len(loads)
        copy = pltpu.make_async_copy(src, dst, in_sem.at[k])
        copy.start()
        loads[name] = copy

    load("e", embed_hbm.at[:, :, cols_a], ewin)
    load("p0", pin_hbm.at[0], wbuf.at[0, pl.ds(0, 3), inner_rows])
    load("h", ho_hbm.at[:, :, cols_a], hwin)
    load("o0", po_hbm.at[0], wbuf.at[0, 3, inner_rows])
    load("p1", pin_hbm.at[1], wbuf.at[1, pl.ds(0, 3), inner_rows])
    load("o1", po_hbm.at[1], wbuf.at[1, 3, inner_rows])
    load("gain", gain_hbm, gain)
    load("gw", gw_hbm, gw)
    fc = D // FEAT_CHUNKS
    for c in range(FEAT_CHUNKS):
        pltpu.make_async_copy(
            feats_hbm.at[0, :, pl.ds(c * fc, fc)], fbuf.at[:, pl.ds(c * fc, fc)], feat_sem.at[c]
        ).start()
    load("es", embed_hbm.at[:, :, cols_s], ewin_s)
    load("hs", ho_hbm.at[:, :, cols_s], hwin_s)
    load("noise", noise_hbm, noise)
    load("qk", qk_hbm, qk_ref)

    if win_a != part:
        pad = pl.ds(pl.multiple_of((part // 64) * 64 - (part // 64) * off_a, 64), 64)
        for n in range(2):
            for j in range(4):
                wbuf[n, j, pad, :] = jnp.zeros((64, wbuf.shape[3]), BF)
    for n in range(2):
        for h in range(2):
            vext[n, h, :, HD:] = jnp.ones((span, HD), BF)

    def place(n, j):
        return j // 2, (2 * n + j % 2) * 2 * chans

    def fuse(n):
        for j in range(4):
            left = ewin if j < 3 else hwin
            x = mm(left[n], wbuf[n, j]).astype(BF)
            g, base = place(n, j)
            wpart[g, base : base + chans, :] = x[:, :HD]
            wpart[g, base + chans : base + 2 * chans, :] = x[:, HD:]

    share = 8 * chans // (L * X)

    def share_rows(peer):
        return pl.ds(pl.multiple_of((peer["level"] * X + peer["dp"]) * share, share), share)

    own_share = share_rows({"level": l, "dp": d})

    def send_shares(n):
        for o, peer in enumerate(team):
            remote(wpart.at[n, share_rows(peer)], rx.at[n, o], s_rx.at[n], r_rx.at[n], peer)

    def sum_shares(n):
        drain(rx.at[n], r_rx.at[n])
        total = wpart[n, own_share, :].astype(F32)
        for o in range(len(team)):
            total = total + rx[n, o].astype(F32)
        wfull[n, own_share, :] = total.astype(BF)
        for peer in team:
            remote(wfull.at[n, own_share], wfull.at[n, own_share], s_ax.at[n], r_ax.at[n], peer)

    def feat_chunk(c):
        cols = pl.ds(c * fc, fc)
        pltpu.make_async_copy(feats_hbm.at[0, :, cols], fbuf.at[:, cols], feat_sem.at[c]).wait()
        scaled = (gw[:, c * fc : (c + 1) * fc].astype(F32) * gain[:, c * fc : (c + 1) * fc]).astype(BF)

        def rows_body(i, _):
            rows = pl.ds(pl.multiple_of(i * 64, 64), 64)
            acc = jnp.zeros((64, 128), F32)
            for k in range(fc // 128):
                x = fbuf[rows, c * fc + k * 128 : c * fc + (k + 1) * 128].astype(F32)
                acc = acc + x * x
            ssq[rows, :] = acc if c == 0 else ssq[rows, :] + acc
            return 0

        lax.fori_loop(0, span // 64, rows_body, 0)
        prod = mm(fbuf[:, c * fc : (c + 1) * fc], scaled, NT)
        x0[...] = prod if c == 0 else x0[...] + prod

    loads["e"].wait()
    loads["h"].wait()
    loads["p0"].wait()
    loads["o0"].wait()
    fuse(0)
    loads["p1"].wait()
    loads["o1"].wait()
    fuse(1)
    loads["gain"].wait()
    loads["gw"].wait()
    feat_chunk(0)
    feat_chunk(1)
    pl.semaphore_wait(barrier, L * X - 1 + 2 * chips - 1)
    send_shares(0)
    send_shares(1)
    for c in range(2, FEAT_CHUNKS):
        feat_chunk(c)

    loads["noise"].wait()
    loads["es"].wait()
    loads["hs"].wait()
    loads["qk"].wait()
    scale = lax.rsqrt(jnp.sum(ssq[...], axis=-1, keepdims=True) * (1.0 / D) + 1e-06)
    rms[...] = jnp.broadcast_to(scale, rms.shape)
    xz = x0[...] * scale
    x0[...] = xz
    sig = jnp.full((1, chans), sigma_ref[0], F32)
    xin[...] = ((xz + sig * noise[...].T) * lax.rsqrt(sig * sig + 1.0)).astype(BF)

    def straight(n):
        e = ewin_s[n]
        if win_s != part_s:
            lane = lax.broadcasted_iota(jnp.int32, (chans, win_s), 1)
            keep = jnp.logical_and(lane >= off_s, lane < off_s + part_s)
            e = jnp.where(keep, e.astype(F32), 0.0).astype(BF)
        return mm(hwin_s[n], e, NT)

    bent = (straight(1) - straight(0)).astype(BF)
    none = jnp.zeros_like(bent)

    def packed(left, rightT):
        blank = jnp.zeros_like(rightT)
        low = mm(left[:half], jnp.concatenate([rightT, blank], axis=0), NT)
        return low + mm(left[half:], jnp.concatenate([blank, rightT], axis=0), NT)

    sum_shares(0)
    sum_shares(1)
    total = packed(xin[...], bent)

    fold = math.log2(math.e) / math.sqrt(HD)
    def matrix(n, j):
        g, base = place(n, j)
        return jnp.concatenate([wfull[g, base + h * chans : base + (h + 1) * chans] for h in range(2)], axis=1)

    def active(rows, mat):
        a = mm(xin[rows, :], mat) * 0.5
        return a * jnp.tanh(a) + a

    drain(rx.at[0], r_ax.at[0])
    for n in range(2):
        for j, buf in enumerate((qbuf, kbuf)):
            mat = matrix(n, j)
            row = qk_ref[2 * n + j : 2 * n + j + 1, :]
            if j == 0:
                row = row * fold
            for i in range(span // 128):
                rows = slice(i * 128, (i + 1) * 128)
                act = active(rows, mat)
                for h in range(2):
                    t = act[:, h * HD : (h + 1) * HD]
                    mean = jnp.mean(t * t, axis=-1, keepdims=True)
                    buf[n, h, rows, :] = (t * lax.rsqrt(mean + 1e-06) * row).astype(BF)
        for b in range(span // QBLOCK):
            rows = slice(b * QBLOCK, (b + 1) * QBLOCK)
            for h in range(2):
                pbuf[n, h, rows, :] = jnp.exp2(mm(qbuf[n, h, rows, :], kbuf[n, h], NT)).astype(BF)
    drain(rx.at[1], r_ax.at[1])
    for n in range(2):
        mat = matrix(n, 2)
        for i in range(span // 128):
            rows = slice(i * 128, (i + 1) * 128)
            act = active(rows, mat)
            for h in range(2):
                vext[n, h, rows, 0:HD] = act[:, h * HD : (h + 1) * HD].astype(BF)
        for b in range(span // QBLOCK):
            rows = slice(b * QBLOCK, (b + 1) * QBLOCK)
            for h in range(2):
                both = mm(pbuf[n, h, rows, :], vext[n, h])
                obuf[n, rows, h * HD : (h + 1) * HD] = (both[:, :HD] / both[:, HD:]).astype(BF)
        field = packed(obuf[n], matrix(n, 3))
        total = total + field if n else total - field

    tsend[...] = (total * lw_ref[0]).astype(BF)
    blocks = chips // 2
    trows = half // blocks

    def block_of(peer):
        return pl.ds(pl.multiple_of((peer["seq"] // 4 * L + peer["level"]) * trows, trows), trows)

    mine_b = block_of({"level": l, "seq": s})
    owner = core == z // L
    spot_b = 2 * (s // 2 * L + l) + core
    for step in steps(range(Z)):
        peer = on_chip(step, None)
        remote(tsend.at[block_of(peer)], b1.at[spot_b], s_b1, r_b1, peer)

    @pl.when(owner)
    def _():
        b1[spot_b] = tsend[mine_b, :]
        drain(b1.at[pl.ds(0, 2 * chips - 1)], r_b1)
        acc = b1[0].astype(F32)
        for i in range(1, 2 * chips):
            acc = acc + b1[i].astype(F32)
        gfull[mine_b, :] = acc.astype(BF)
        for peer in [on_chip(step, c) for step in steps((0, 1, 2, Z - 1)) for c in range(2)] + [{"seq": mate}]:
            remote(gfull.at[mine_b], gfull.at[mine_b], s_b3, r_b3, peer)
        drain(b1.at[pl.ds(0, blocks - 1)], r_b3)

    @pl.when(jnp.logical_not(owner))
    def _():
        remote(tsend.at[mine_b], b1.at[spot_b], s_b1, r_b1, {"seq": mate})
        drain(b1.at[pl.ds(0, blocks)], r_b3)

    cut = D // X
    side = cut // 2
    lane = lax.broadcasted_iota(jnp.int32, (half, 2 * chans), 1)
    scaling = jnp.where(lane < chans, rms[0:half, :], rms[half:, :])
    turned = (gfull[...].astype(F32) * scaling).T.astype(BF)
    for o in ((2, 1, 3) if X == 4 else tuple(range(1, X))) + (0,):
        to = lax.rem(d + o, X)
        cols = pl.ds(pl.multiple_of(to * cut + core * side, 128), side)
        term = mm(turned[:chans], fbuf[0:half, cols]) + mm(turned[chans:], fbuf[half:, cols])
        if o:
            psend[o - 1] = term.astype(BF)
            remote(psend.at[o - 1], crecv.at[d], s_c, r_c, {"dp": to})
        else:
            crecv[d] = term.astype(BF)

    rows_h = span // S
    first = s * rows_h
    which = first // half
    own = pl.ds(pl.multiple_of(first, rows_h), rows_h)
    g_own = gfull[pl.ds(pl.multiple_of(first - which * half, rows_h), rows_h), :].astype(F32)
    g_own = jnp.where(which == 0, g_own, pltpu.roll(g_own, chans, 1))[:, :chans]
    inner = jnp.sum(g_own * x0[own, :], axis=-1, keepdims=True) * (1.0 / D)
    scale_own = rms[own, 0:1]
    lessen = scale_own * inner
    g_own = g_own.astype(BF)
    for c in range(FEAT_CHUNKS):
        cols = slice(c * fc, (c + 1) * fc)
        grad = mm(g_own, gw[:, cols]) * gain[:, cols] - fbuf[own, cols].astype(F32) * lessen
        oh_ref[:, cols] = (grad * scale_own).astype(BF)

    drain(crecv.at[pl.ds(0, X - 1)], r_c)
    acc = crecv[0].astype(F32)
    for i in range(1, X):
        acc = acc + crecv[i].astype(F32)
    factor = 1.0 / math.sqrt(X * span)
    mine = pl.ds(pl.multiple_of(d * cut + core * side, 128), side)
    spot = pl.ds(pl.multiple_of(core * side, 128), side)
    ow_ref[:, spot] = acc * (gain[:, mine] * factor)
    remote(ow_ref.at[:, spot], ow_ref.at[:, spot], s_k, r_k, {"seq": mate})
    drain(psend, s_c)
    for n in range(2):
        drain(rx.at[n], s_rx.at[n])
        drain(rx.at[n], s_ax.at[n])
    drain(b1.at[pl.ds(0, chips - 1)], s_b1)

    @pl.when(owner)
    def _():
        drain(b1.at[pl.ds(0, 2 * blocks - 1)], s_b3)

    @pl.when(jnp.logical_not(owner))
    def _():
        drain(b1.at[0], s_b1)


    drain(ow_ref.at[:, 0:side], r_k)
    block = pl.ds(pl.multiple_of(d * cut, 128), cut)
    inside = jnp.sum(ow_ref[...] * gw[:, block].astype(F32), axis=0, keepdims=True)
    og_ref[...] = inside / gain[:, block]
    drain(ow_ref.at[:, 0:side], s_k)


def on_device(feats, gen_gain, gen_weight, noise, sigmas, level_weights, embed, proj_in, proj_out, head_out, qk_gain):
    sizes = L, S, X = tuple(lax.axis_size(a) for a in ("level", "seq", "dp"))
    span, D = feats.shape[1:]
    chans = gen_weight.shape[1]
    part = proj_in.shape[2]
    win_a = part if part % 128 == 0 else part + 64
    win_s = D // S if D // S % 128 == 0 else D // S + 64
    half = span // 2
    side = D // X // 2
    rows_h = span // S
    hbm = pl.BlockSpec(memory_space=pltpu.HBM)
    vmem = pl.BlockSpec(memory_space=pltpu.VMEM)
    smem = pl.BlockSpec(memory_space=pltpu.SMEM)
    V = pltpu.VMEM
    dma = pltpu.SemaphoreType.DMA
    scratch = [
        V((4, HD), F32),
        V((span, D), BF), V((1, D), F32), V((chans, D), BF), V((chans, span), F32),
        V((2, chans, win_a), BF), V((2, chans, win_a), BF), V((2, chans, win_s), BF), V((2, chans, win_s), BF),
        V((2, 4, win_a, 2 * HD), BF),
        V((2, 8 * chans, HD), BF), V((2, L * X - 1, 8 * chans // (L * X), HD), BF), V((2, 8 * chans, HD), BF),
        V((span, 128), F32), V((span, chans), F32), V((span, 128), F32), V((span, chans), BF),
        V((2, 2, span, HD), BF), V((2, 2, span, HD), BF), V((2, 2, span, span), BF),
        V((2, 2, span, 2 * HD), BF), V((2, span, 2 * HD), BF),
        V((half, 2 * chans), BF), V((L * S, 4 * half // (L * S), 2 * chans), BF),
        V((half, 2 * chans), BF), V((X - 1, chans, side), BF), V((X, chans, side), BF),
        dma((12,)), dma((FEAT_CHUNKS,)),
    ] + [dma((2,))] * 4 + [dma] * 8
    out_h, out_w, out_g = pl.pallas_call(
        functools.partial(kernel, sizes),
        out_shape=(
            V((rows_h, D), BF),
            V((chans, 2 * side), F32),
            V((1, 2 * side), F32),
        ),
        in_specs=[smem] * 2 + [hbm] * 9,
        out_specs=(vmem, vmem, vmem),
        scratch_shapes=scratch,
        compiler_params=pltpu.CompilerParams(
            collective_id=0, has_side_effects=True, vmem_limit_bytes=40 * 1024 * 1024
        ),
    )(
        sigmas,
        level_weights,
        *(
            pltpu.with_memory_space_constraint(a, pltpu.HBM)
            for a in (
                qk_gain.reshape(4, HD), feats, gen_gain[None], gen_weight.T, noise[0, 0].T,
                embed, proj_in, jnp.swapaxes(proj_out, 1, 2), jnp.swapaxes(head_out, 1, 2),
            )
        ),
    )
    return out_h[None], out_w.T, out_g[0]


def solution(mesh):
    in_specs = (
        P("dp", None, None),
        P(),
        P(),
        P("level", "dp", None, None),
        P("level"),
        P("level"),
        P(),
        P(None, None, ("level", "dp"), "seq"),
        P(None, "seq", ("level", "dp")),
        P(),
        P(),
    )
    out_specs = (P("dp", "seq", None), P("dp", None), P("dp"))
    return jax.shard_map(on_device, mesh=mesh, in_specs=in_specs, out_specs=out_specs, check_vma=False)
```

```python
import functools
import math

import jax
import jax.numpy as jnp
from jax import lax
from jax.experimental import pallas as pl
from jax.experimental.pallas import tpu as pltpu
from jax.sharding import PartitionSpec as P

HD = 128
BF = jnp.bfloat16
F32 = jnp.float32
MESH = pl.DeviceIdType.MESH
NT = (((1,), (1,)), ((), ()))
NN = (((1,), (0,)), ((), ()))
FEAT_CHUNKS = 5
QBLOCK = 256


def mm(a, b, dims=NN):
    return lax.dot_general(a, b, dims, preferred_element_type=F32)


def window(index, part):
    if part % 128 == 0:
        return index * part, part, 0
    assert part % 128 == 64
    offset = lax.rem(index, 2) * 64
    return index * part - offset, part + 64, offset


def kernel(
    sizes,
    sigma_ref, lw_ref, qk_hbm, feats_hbm, gain_hbm, gw_hbm, noise_hbm, embed_hbm, pin_hbm, po_hbm, ho_hbm,
    oh_ref, ow_ref, og_ref,
    qk_ref, fbuf, gain, gw, noise, ewin, hwin, ewin_s, hwin_s, wbuf,
    wpart, rx, wfull,
    ssq, x0, rms, xin, qbuf, kbuf, pbuf, vext, obuf,
    tsend, b1, gfull, psend, crecv,
    in_sem, feat_sem,
    s_rx, r_rx, s_ax, r_ax,
    s_b1, r_b1, s_b3, r_b3, s_c, r_c, s_k, r_k,
):
    L, S, X = sizes
    D = fbuf.shape[1]
    span = fbuf.shape[0]
    chans = gw.shape[0]
    half = span // 2
    l, s, d = lax.axis_index("level"), lax.axis_index("seq"), lax.axis_index("dp")
    core = lax.rem(s, 2)
    mate = s + 1 - 2 * core

    mirror = [l, l + 1 - 2 * lax.rem(l, 2), l + 2 - 4 * (l // 2), L - 1 - l]
    team = [
        {"level": mirror[a], "dp": lax.rem(d + b, X)} for a in (3, 2, 1, 0) for b in (2, 1, 3, 0) if a or b
    ]
    away = [{"level": mirror[a], "dp": lax.rem(d + b, X)} for a in (3, 2, 1, 0) for b in (2, 1, 3)]
    Z, Y = 2 * L, S // 4
    chips = Z * Y
    y, z = s // 4, lax.rem(s // 2, 2) * L + l

    def steps(steps_z):
        far = lambda step: min(step[0], Y - step[0]) + min(step[1], Z - step[1])
        return sorted([(a, b) for a in range(Y) for b in steps_z if a or b], key=far, reverse=True)

    def chip(step):
        to_y, to_z = lax.rem(y + step[0], Y), lax.rem(z + step[1], Z)
        return lax.rem(to_z, L), 4 * to_y + 2 * (to_z // L), to_z // L

    def on_chip(step, of_core):
        to_level, to_seq, z_hi = chip(step)
        return {"level": to_level, "seq": to_seq + (z_hi if of_core is None else of_core)}

    def remote(src, dst, ssem, rsem, where):
        copy = pltpu.make_async_remote_copy(
            src_ref=src, dst_ref=dst, send_sem=ssem, recv_sem=rsem, device_id=where, device_id_type=MESH
        )
        copy.start()
        return copy

    def drain(ref, sem):
        pltpu.make_async_copy(ref, ref, sem).wait()

    barrier = pltpu.get_barrier_semaphore()
    for peer in [on_chip(step, c) for step in steps(range(Z)) for c in range(2)] + away + [{"seq": mate}]:
        pl.semaphore_signal(barrier, inc=1, device_id=peer, device_id_type=MESH)

    part = pin_hbm.shape[2]
    start_a, win_a, off_a = window(l * X + d, part)
    part_s = D // S
    start_s, win_s, off_s = window(s, part_s)
    if win_a != part:
        start_a = pl.multiple_of(start_a, 128)
        off_a = pl.multiple_of(off_a, 64)
    if win_s != part_s:
        start_s = pl.multiple_of(start_s, 128)
    cols_a, cols_s = pl.ds(start_a, win_a), pl.ds(start_s, win_s)
    inner_rows = pl.ds(off_a, part)

    loads = {}

    def load(name, src, dst):
        k = len(loads)
        copy = pltpu.make_async_copy(src, dst, in_sem.at[k])
        copy.start()
        loads[name] = copy

    load("e", embed_hbm.at[:, :, cols_a], ewin)
    load("p0", pin_hbm.at[0], wbuf.at[0, pl.ds(0, 3), inner_rows])
    load("h", ho_hbm.at[:, :, cols_a], hwin)
    load("o0", po_hbm.at[0], wbuf.at[0, 3, inner_rows])
    load("p1", pin_hbm.at[1], wbuf.at[1, pl.ds(0, 3), inner_rows])
    load("o1", po_hbm.at[1], wbuf.at[1, 3, inner_rows])
    load("gain", gain_hbm, gain)
    load("gw", gw_hbm, gw)
    fc = D // FEAT_CHUNKS
    for c in range(FEAT_CHUNKS):
        pltpu.make_async_copy(
            feats_hbm.at[0, :, pl.ds(c * fc, fc)], fbuf.at[:, pl.ds(c * fc, fc)], feat_sem.at[c]
        ).start()
    load("es", embed_hbm.at[:, :, cols_s], ewin_s)
    load("hs", ho_hbm.at[:, :, cols_s], hwin_s)
    load("noise", noise_hbm, noise)
    load("qk", qk_hbm, qk_ref)

    if win_a != part:
        pad = pl.ds(pl.multiple_of((part // 64) * 64 - (part // 64) * off_a, 64), 64)
        for n in range(2):
            for j in range(4):
                wbuf[n, j, pad, :] = jnp.zeros((64, wbuf.shape[3]), BF)
    for n in range(2):
        for h in range(2):
            vext[n, h, :, HD:] = jnp.ones((span, HD), BF)

    def place(n, j):
        return j // 2, (2 * n + j % 2) * 2 * chans

    def fuse(n):
        for j in range(4):
            left = ewin if j < 3 else hwin
            x = mm(left[n], wbuf[n, j]).astype(BF)
            g, base = place(n, j)
            wpart[g, base : base + chans, :] = x[:, :HD]
            wpart[g, base + chans : base + 2 * chans, :] = x[:, HD:]

    share = 8 * chans // (L * X)

    def share_rows(peer):
        return pl.ds(pl.multiple_of((peer["level"] * X + peer["dp"]) * share, share), share)

    own_share = share_rows({"level": l, "dp": d})

    def send_shares(n):
        for o, peer in enumerate(team):
            remote(wpart.at[n, share_rows(peer)], rx.at[n, o], s_rx.at[n], r_rx.at[n], peer)

    def sum_shares(n):
        drain(rx.at[n], r_rx.at[n])
        total = wpart[n, own_share, :].astype(F32)
        for o in range(len(team)):
            total = total + rx[n, o].astype(F32)
        wfull[n, own_share, :] = total.astype(BF)
        for peer in team:
            remote(wfull.at[n, own_share], wfull.at[n, own_share], s_ax.at[n], r_ax.at[n], peer)

    def feat_chunk(c):
        cols = pl.ds(c * fc, fc)
        pltpu.make_async_copy(feats_hbm.at[0, :, cols], fbuf.at[:, cols], feat_sem.at[c]).wait()
        scaled = (gw[:, c * fc : (c + 1) * fc].astype(F32) * gain[:, c * fc : (c + 1) * fc]).astype(BF)

        def rows_body(i, _):
            rows = pl.ds(pl.multiple_of(i * 64, 64), 64)
            acc = jnp.zeros((64, 128), F32)
            for k in range(fc // 128):
                x = fbuf[rows, c * fc + k * 128 : c * fc + (k + 1) * 128].astype(F32)
                acc = acc + x * x
            ssq[rows, :] = acc if c == 0 else ssq[rows, :] + acc
            return 0

        lax.fori_loop(0, span // 64, rows_body, 0)
        prod = mm(fbuf[:, c * fc : (c + 1) * fc], scaled, NT)
        x0[...] = prod if c == 0 else x0[...] + prod

    loads["e"].wait()
    loads["h"].wait()
    loads["p0"].wait()
    loads["o0"].wait()
    fuse(0)
    loads["p1"].wait()
    loads["o1"].wait()
    fuse(1)
    loads["gain"].wait()
    loads["gw"].wait()
    feat_chunk(0)
    feat_chunk(1)
    pl.semaphore_wait(barrier, L * (X - 1) + 2 * chips - 1)
    send_shares(0)
    send_shares(1)
    for c in range(2, FEAT_CHUNKS):
        feat_chunk(c)

    loads["noise"].wait()
    loads["es"].wait()
    loads["hs"].wait()
    loads["qk"].wait()
    scale = lax.rsqrt(jnp.sum(ssq[...], axis=-1, keepdims=True) * (1.0 / D) + 1e-06)
    rms[...] = jnp.broadcast_to(scale, rms.shape)
    xz = x0[...] * scale
    x0[...] = xz
    sig = jnp.full((1, chans), sigma_ref[0], F32)
    xin[...] = ((xz + sig * noise[...].T) * lax.rsqrt(sig * sig + 1.0)).astype(BF)

    def straight(n):
        e = ewin_s[n]
        if win_s != part_s:
            lane = lax.broadcasted_iota(jnp.int32, (chans, win_s), 1)
            keep = jnp.logical_and(lane >= off_s, lane < off_s + part_s)
            e = jnp.where(keep, e.astype(F32), 0.0).astype(BF)
        return mm(hwin_s[n], e, NT)

    bent = (straight(1) - straight(0)).astype(BF)
    none = jnp.zeros_like(bent)

    def packed(left, rightT):
        blank = jnp.zeros_like(rightT)
        low = mm(left[:half], jnp.concatenate([rightT, blank], axis=0), NT)
        return low + mm(left[half:], jnp.concatenate([blank, rightT], axis=0), NT)

    sum_shares(0)
    sum_shares(1)
    total = packed(xin[...], bent)

    fold = math.log2(math.e) / math.sqrt(HD)
    def matrix(n, j):
        g, base = place(n, j)
        return jnp.concatenate([wfull[g, base + h * chans : base + (h + 1) * chans] for h in range(2)], axis=1)

    def active(rows, mat):
        a = mm(xin[rows, :], mat) * 0.5
        return a * jnp.tanh(a) + a

    drain(rx.at[0], r_ax.at[0])
    for n in range(2):
        for j, buf in enumerate((qbuf, kbuf)):
            mat = matrix(n, j)
            row = qk_ref[2 * n + j : 2 * n + j + 1, :]
            if j == 0:
                row = row * fold
            for i in range(span // 128):
                rows = slice(i * 128, (i + 1) * 128)
                act = active(rows, mat)
                for h in range(2):
                    t = act[:, h * HD : (h + 1) * HD]
                    mean = jnp.mean(t * t, axis=-1, keepdims=True)
                    buf[n, h, rows, :] = (t * lax.rsqrt(mean + 1e-06) * row).astype(BF)
        for b in range(span // QBLOCK):
            rows = slice(b * QBLOCK, (b + 1) * QBLOCK)
            for h in range(2):
                pbuf[n, h, rows, :] = jnp.exp2(mm(qbuf[n, h, rows, :], kbuf[n, h], NT)).astype(BF)
    drain(rx.at[1], r_ax.at[1])
    for n in range(2):
        mat = matrix(n, 2)
        for i in range(span // 128):
            rows = slice(i * 128, (i + 1) * 128)
            act = active(rows, mat)
            for h in range(2):
                vext[n, h, rows, 0:HD] = act[:, h * HD : (h + 1) * HD].astype(BF)
        for b in range(span // QBLOCK):
            rows = slice(b * QBLOCK, (b + 1) * QBLOCK)
            for h in range(2):
                both = mm(pbuf[n, h, rows, :], vext[n, h])
                obuf[n, rows, h * HD : (h + 1) * HD] = (both[:, :HD] / both[:, HD:]).astype(BF)
        field = packed(obuf[n], matrix(n, 3))
        total = total + field if n else total - field

    tsend[...] = (total * lw_ref[0]).astype(BF)
    blocks = chips // 2
    trows = half // blocks

    def block_of(peer):
        return pl.ds(pl.multiple_of((peer["seq"] // 4 * L + peer["level"]) * trows, trows), trows)

    mine_b = block_of({"level": l, "seq": s})
    owner = core == z // L
    spot_b = 2 * (s // 2 * L + l) + core
    for step in steps(range(Z)):
        peer = on_chip(step, None)
        remote(tsend.at[block_of(peer)], b1.at[spot_b], s_b1, r_b1, peer)

    @pl.when(owner)
    def _():
        b1[spot_b] = tsend[mine_b, :]
        drain(b1.at[pl.ds(0, 2 * chips - 1)], r_b1)
        acc = b1[0].astype(F32)
        for i in range(1, 2 * chips):
            acc = acc + b1[i].astype(F32)
        gfull[mine_b, :] = acc.astype(BF)
        for peer in [on_chip(step, c) for step in steps((0, 1, 2, Z - 1)) for c in range(2)] + [{"seq": mate}]:
            remote(gfull.at[mine_b], gfull.at[mine_b], s_b3, r_b3, peer)
        drain(b1.at[pl.ds(0, blocks - 1)], r_b3)

    @pl.when(jnp.logical_not(owner))
    def _():
        remote(tsend.at[mine_b], b1.at[spot_b], s_b1, r_b1, {"seq": mate})
        drain(b1.at[pl.ds(0, blocks)], r_b3)

    cut = D // X
    side = cut // 2
    lane = lax.broadcasted_iota(jnp.int32, (half, 2 * chans), 1)
    scaling = jnp.where(lane < chans, rms[0:half, :], rms[half:, :])
    turned = (gfull[...].astype(F32) * scaling).T.astype(BF)
    for o in ((2, 1, 3) if X == 4 else tuple(range(1, X))) + (0,):
        to = lax.rem(d + o, X)
        cols = pl.ds(pl.multiple_of(to * cut + core * side, 128), side)
        term = mm(turned[:chans], fbuf[0:half, cols]) + mm(turned[chans:], fbuf[half:, cols])
        if o:
            psend[o - 1] = term.astype(BF)
            remote(psend.at[o - 1], crecv.at[d], s_c, r_c, {"dp": to})
        else:
            crecv[d] = term.astype(BF)

    rows_h = span // S
    first = s * rows_h
    which = first // half
    own = pl.ds(pl.multiple_of(first, rows_h), rows_h)
    g_own = gfull[pl.ds(pl.multiple_of(first - which * half, rows_h), rows_h), :].astype(F32)
    g_own = jnp.where(which == 0, g_own, pltpu.roll(g_own, chans, 1))[:, :chans]
    inner = jnp.sum(g_own * x0[own, :], axis=-1, keepdims=True) * (1.0 / D)
    scale_own = rms[own, 0:1]
    lessen = scale_own * inner
    g_own = g_own.astype(BF)
    for c in range(FEAT_CHUNKS):
        cols = slice(c * fc, (c + 1) * fc)
        grad = mm(g_own, gw[:, cols]) * gain[:, cols] - fbuf[own, cols].astype(F32) * lessen
        oh_ref[:, cols] = (grad * scale_own).astype(BF)

    drain(crecv.at[pl.ds(0, X - 1)], r_c)
    acc = crecv[0].astype(F32)
    for i in range(1, X):
        acc = acc + crecv[i].astype(F32)
    factor = 1.0 / math.sqrt(X * span)
    mine = pl.ds(pl.multiple_of(d * cut + core * side, 128), side)
    spot = pl.ds(pl.multiple_of(core * side, 128), side)
    ow_ref[:, spot] = acc * (gain[:, mine] * factor)
    remote(ow_ref.at[:, spot], ow_ref.at[:, spot], s_k, r_k, {"seq": mate})
    drain(psend, s_c)
    for n in range(2):
        drain(rx.at[n], s_rx.at[n])
        drain(rx.at[n], s_ax.at[n])
    drain(b1.at[pl.ds(0, chips - 1)], s_b1)

    @pl.when(owner)
    def _():
        drain(b1.at[pl.ds(0, 2 * blocks - 1)], s_b3)

    @pl.when(jnp.logical_not(owner))
    def _():
        drain(b1.at[0], s_b1)


    drain(ow_ref.at[:, 0:side], r_k)
    block = pl.ds(pl.multiple_of(d * cut, 128), cut)
    inside = jnp.sum(ow_ref[...] * gw[:, block].astype(F32), axis=0, keepdims=True)
    og_ref[...] = (inside / gain[:, block])[0]
    drain(ow_ref.at[:, 0:side], s_k)


def on_device(feats, gen_gain, gen_weight, noise, sigmas, level_weights, embed, proj_in, proj_out, head_out, qk_gain):
    sizes = L, S, X = tuple(lax.axis_size(a) for a in ("level", "seq", "dp"))
    span, D = feats.shape[1:]
    chans = gen_weight.shape[1]
    part = proj_in.shape[2]
    win_a = part if part % 128 == 0 else part + 64
    win_s = D // S if D // S % 128 == 0 else D // S + 64
    half = span // 2
    side = D // X // 2
    rows_h = span // S
    hbm = pl.BlockSpec(memory_space=pltpu.HBM)
    vmem = pl.BlockSpec(memory_space=pltpu.VMEM)
    smem = pl.BlockSpec(memory_space=pltpu.SMEM)
    V = pltpu.VMEM
    dma = pltpu.SemaphoreType.DMA
    scratch = [
        V((4, HD), F32),
        V((span, D), BF), V((1, D), F32), V((chans, D), BF), V((chans, span), F32),
        V((2, chans, win_a), BF), V((2, chans, win_a), BF), V((2, chans, win_s), BF), V((2, chans, win_s), BF),
        V((2, 4, win_a, 2 * HD), BF),
        V((2, 8 * chans, HD), BF), V((2, L * X - 1, 8 * chans // (L * X), HD), BF), V((2, 8 * chans, HD), BF),
        V((span, 128), F32), V((span, chans), F32), V((span, 128), F32), V((span, chans), BF),
        V((2, 2, span, HD), BF), V((2, 2, span, HD), BF), V((2, 2, span, span), BF),
        V((2, 2, span, 2 * HD), BF), V((2, span, 2 * HD), BF),
        V((half, 2 * chans), BF), V((L * S, 4 * half // (L * S), 2 * chans), BF),
        V((half, 2 * chans), BF), V((X - 1, chans, side), BF), V((X, chans, side), BF),
        dma((12,)), dma((FEAT_CHUNKS,)),
    ] + [dma((2,))] * 4 + [dma] * 8
    out_h, out_w, out_g = pl.pallas_call(
        functools.partial(kernel, sizes),
        out_shape=(
            V((rows_h, D), BF),
            V((chans, 2 * side), F32),
            V((2 * side,), F32),
        ),
        in_specs=[smem] * 2 + [hbm] * 9,
        out_specs=(vmem, vmem, vmem),
        scratch_shapes=scratch,
        compiler_params=pltpu.CompilerParams(
            collective_id=0, has_side_effects=True, vmem_limit_bytes=40 * 1024 * 1024
        ),
    )(
        sigmas,
        level_weights,
        *(
            pltpu.with_memory_space_constraint(a, pltpu.HBM)
            for a in (
                qk_gain.reshape(4, HD), feats, gen_gain[None], gen_weight.T, noise[0, 0].T,
                embed, proj_in, jnp.swapaxes(proj_out, 1, 2), jnp.swapaxes(head_out, 1, 2),
            )
        ),
    )
    return out_h[None], out_w.T, out_g


def solution(mesh):
    in_specs = (
        P("dp", None, None),
        P(),
        P(),
        P("level", "dp", None, None),
        P("level"),
        P("level"),
        P(),
        P(None, None, ("level", "dp"), "seq"),
        P(None, "seq", ("level", "dp")),
        P(),
        P(),
    )
    out_specs = (P("dp", "seq", None), P("dp", None), P("dp"))
    return jax.shard_map(on_device, mesh=mesh, in_specs=in_specs, out_specs=out_specs, check_vma=False)
```

```python
import functools
import math

import jax
import jax.numpy as jnp
from jax import lax
from jax.experimental import pallas as pl
from jax.experimental.pallas import tpu as pltpu
from jax.sharding import PartitionSpec as P

HD = 128
BF = jnp.bfloat16
F32 = jnp.float32
MESH = pl.DeviceIdType.MESH
NT = (((1,), (1,)), ((), ()))
NN = (((1,), (0,)), ((), ()))
FEAT_CHUNKS = 5
QBLOCK = 256


def mm(a, b, dims=NN):
    return lax.dot_general(a, b, dims, preferred_element_type=F32)


def window(index, part):
    if part % 128 == 0:
        return index * part, part, 0
    assert part % 128 == 64
    offset = lax.rem(index, 2) * 64
    return index * part - offset, part + 64, offset


def kernel(
    sizes,
    sigma_ref, lw_ref, qk_hbm, feats_hbm, gain_hbm, gw_hbm, noise_hbm, embed_hbm, pin_hbm, po_hbm, ho_hbm,
    oh_ref, ow_ref, og_ref,
    qk_ref, fbuf, gain, gw, noise, ewin, hwin, ewin_s, hwin_s, wbuf,
    wpart, rx, wfull,
    ssq, x0, rms, xin, qbuf, kbuf, pbuf, vext, obuf,
    tsend, b1, gfull, psend, crecv,
    in_sem, feat_sem,
    s_rx, r_rx, s_ax, r_ax,
    s_b1, r_b1, s_b3, r_b3, s_c, r_c, s_k, r_k,
):
    L, S, X = sizes
    D = fbuf.shape[1]
    span = fbuf.shape[0]
    chans = gw.shape[0]
    half = span // 2
    l, s, d = lax.axis_index("level"), lax.axis_index("seq"), lax.axis_index("dp")
    core = lax.rem(s, 2)
    mate = s + 1 - 2 * core

    mirror = [l, l + 1 - 2 * lax.rem(l, 2), l + 2 - 4 * (l // 2), L - 1 - l]
    team = [
        {"level": mirror[a], "dp": lax.rem(d + b, X)} for a in (3, 2, 1, 0) for b in (2, 1, 3, 0) if a or b
    ]
    away = [{"level": mirror[a], "dp": lax.rem(d + b, X)} for a in (3, 2, 1, 0) for b in (2, 1, 3)]
    Z, Y = 2 * L, S // 4
    chips = Z * Y
    y, z = s // 4, lax.rem(s // 2, 2) * L + l

    def steps(steps_z):
        far = lambda step: min(step[0], Y - step[0]) + min(step[1], Z - step[1])
        return sorted([(a, b) for a in range(Y) for b in steps_z if a or b], key=far, reverse=True)

    def chip(step):
        to_y, to_z = lax.rem(y + step[0], Y), lax.rem(z + step[1], Z)
        return lax.rem(to_z, L), 4 * to_y + 2 * (to_z // L), to_z // L

    def on_chip(step, of_core):
        to_level, to_seq, z_hi = chip(step)
        return {"level": to_level, "seq": to_seq + (z_hi if of_core is None else of_core)}

    def remote(src, dst, ssem, rsem, where):
        copy = pltpu.make_async_remote_copy(
            src_ref=src, dst_ref=dst, send_sem=ssem, recv_sem=rsem, device_id=where, device_id_type=MESH
        )
        copy.start()
        return copy

    def drain(ref, sem):
        pltpu.make_async_copy(ref, ref, sem).wait()

    barrier = pltpu.get_barrier_semaphore()
    for peer in [on_chip(step, c) for step in steps(range(Z)) for c in range(2)] + away + [{"seq": mate}]:
        pl.semaphore_signal(barrier, inc=1, device_id=peer, device_id_type=MESH)

    part = pin_hbm.shape[2]
    start_a, win_a, off_a = window(l * X + d, part)
    part_s = D // S
    start_s, win_s, off_s = window(s, part_s)
    if win_a != part:
        start_a = pl.multiple_of(start_a, 128)
        off_a = pl.multiple_of(off_a, 64)
    if win_s != part_s:
        start_s = pl.multiple_of(start_s, 128)
    cols_a, cols_s = pl.ds(start_a, win_a), pl.ds(start_s, win_s)
    inner_rows = pl.ds(off_a, part)

    loads = {}

    def load(name, src, dst):
        k = len(loads)
        copy = pltpu.make_async_copy(src, dst, in_sem.at[k])
        copy.start()
        loads[name] = copy

    load("e", embed_hbm.at[:, :, cols_a], ewin)
    load("p0", pin_hbm.at[0], wbuf.at[0, pl.ds(0, 3), inner_rows])
    load("h", ho_hbm.at[:, :, cols_a], hwin)
    load("o0", po_hbm.at[0], wbuf.at[0, 3, inner_rows])
    load("p1", pin_hbm.at[1], wbuf.at[1, pl.ds(0, 3), inner_rows])
    load("o1", po_hbm.at[1], wbuf.at[1, 3, inner_rows])
    load("gain", gain_hbm, gain)
    load("gw", gw_hbm, gw)
    fc = D // FEAT_CHUNKS
    for c in range(FEAT_CHUNKS):
        pltpu.make_async_copy(
            feats_hbm.at[0, :, pl.ds(c * fc, fc)], fbuf.at[:, pl.ds(c * fc, fc)], feat_sem.at[c]
        ).start()
    load("es", embed_hbm.at[:, :, cols_s], ewin_s)
    load("hs", ho_hbm.at[:, :, cols_s], hwin_s)
    load("noise", noise_hbm, noise)
    load("qk", qk_hbm, qk_ref)

    if win_a != part:
        pad = pl.ds(pl.multiple_of((part // 64) * 64 - (part // 64) * off_a, 64), 64)
        for n in range(2):
            for j in range(4):
                wbuf[n, j, pad, :] = jnp.zeros((64, wbuf.shape[3]), BF)
    for n in range(2):
        for h in range(2):
            vext[n, h, :, HD:] = jnp.ones((span, HD), BF)

    def place(n, j):
        return j // 2, (2 * n + j % 2) * 2 * chans

    def fuse(n):
        for j in range(4):
            left = ewin if j < 3 else hwin
            x = mm(left[n], wbuf[n, j]).astype(BF)
            g, base = place(n, j)
            wpart[g, base : base + chans, :] = x[:, :HD]
            wpart[g, base + chans : base + 2 * chans, :] = x[:, HD:]

    share = 8 * chans // (L * X)

    def share_rows(peer):
        return pl.ds(pl.multiple_of((peer["level"] * X + peer["dp"]) * share, share), share)

    own_share = share_rows({"level": l, "dp": d})

    def send_shares(n):
        for o, peer in enumerate(team):
            remote(wpart.at[n, share_rows(peer)], rx.at[n, o], s_rx.at[n], r_rx.at[n], peer)

    def sum_shares(n):
        drain(rx.at[n], r_rx.at[n])
        total = wpart[n, own_share, :].astype(F32)
        for o in range(len(team)):
            total = total + rx[n, o].astype(F32)
        wfull[n, own_share, :] = total.astype(BF)
        for peer in team:
            remote(wfull.at[n, own_share], wfull.at[n, own_share], s_ax.at[n], r_ax.at[n], peer)

    def feat_chunk(c):
        cols = pl.ds(c * fc, fc)
        pltpu.make_async_copy(feats_hbm.at[0, :, cols], fbuf.at[:, cols], feat_sem.at[c]).wait()
        scaled = (gw[:, c * fc : (c + 1) * fc].astype(F32) * gain[:, c * fc : (c + 1) * fc]).astype(BF)

        def rows_body(i, _):
            rows = pl.ds(pl.multiple_of(i * 64, 64), 64)
            acc = jnp.zeros((64, 128), F32)
            for k in range(fc // 128):
                x = fbuf[rows, c * fc + k * 128 : c * fc + (k + 1) * 128].astype(F32)
                acc = acc + x * x
            ssq[rows, :] = acc if c == 0 else ssq[rows, :] + acc
            return 0

        lax.fori_loop(0, span // 64, rows_body, 0, unroll=True)
        prod = mm(fbuf[:, c * fc : (c + 1) * fc], scaled, NT)
        x0[...] = prod if c == 0 else x0[...] + prod

    loads["e"].wait()
    loads["h"].wait()
    loads["p0"].wait()
    loads["o0"].wait()
    fuse(0)
    loads["p1"].wait()
    loads["o1"].wait()
    fuse(1)
    loads["gain"].wait()
    loads["gw"].wait()
    feat_chunk(0)
    feat_chunk(1)
    pl.semaphore_wait(barrier, L * (X - 1) + 2 * chips - 1)
    send_shares(0)
    send_shares(1)
    for c in range(2, FEAT_CHUNKS):
        feat_chunk(c)

    loads["noise"].wait()
    loads["es"].wait()
    loads["hs"].wait()
    loads["qk"].wait()
    scale = lax.rsqrt(jnp.sum(ssq[...], axis=-1, keepdims=True) * (1.0 / D) + 1e-06)
    rms[...] = jnp.broadcast_to(scale, rms.shape)
    xz = x0[...] * scale
    x0[...] = xz
    sig = jnp.full((1, chans), sigma_ref[0], F32)
    xin[...] = ((xz + sig * noise[...].T) * lax.rsqrt(sig * sig + 1.0)).astype(BF)

    def straight(n):
        e = ewin_s[n]
        if win_s != part_s:
            lane = lax.broadcasted_iota(jnp.int32, (chans, win_s), 1)
            keep = jnp.logical_and(lane >= off_s, lane < off_s + part_s)
            e = jnp.where(keep, e.astype(F32), 0.0).astype(BF)
        return mm(hwin_s[n], e, NT)

    bent = (straight(1) - straight(0)).astype(BF)
    none = jnp.zeros_like(bent)

    def packed(left, rightT):
        blank = jnp.zeros_like(rightT)
        low = mm(left[:half], jnp.concatenate([rightT, blank], axis=0), NT)
        return low + mm(left[half:], jnp.concatenate([blank, rightT], axis=0), NT)

    sum_shares(0)
    sum_shares(1)
    total = packed(xin[...], bent)

    fold = math.log2(math.e) / math.sqrt(HD)
    def matrix(n, j):
        g, base = place(n, j)
        return jnp.concatenate([wfull[g, base + h * chans : base + (h + 1) * chans] for h in range(2)], axis=1)

    def active(rows, mat):
        a = mm(xin[rows, :], mat) * 0.5
        return a * jnp.tanh(a) + a

    drain(rx.at[0], r_ax.at[0])
    for n in range(2):
        for j, buf in enumerate((qbuf, kbuf)):
            mat = matrix(n, j)
            row = qk_ref[2 * n + j : 2 * n + j + 1, :]
            if j == 0:
                row = row * fold
            for i in range(span // 128):
                rows = slice(i * 128, (i + 1) * 128)
                act = active(rows, mat)
                for h in range(2):
                    t = act[:, h * HD : (h + 1) * HD]
                    mean = jnp.mean(t * t, axis=-1, keepdims=True)
                    buf[n, h, rows, :] = (t * lax.rsqrt(mean + 1e-06) * row).astype(BF)
        for b in range(span // QBLOCK):
            rows = slice(b * QBLOCK, (b + 1) * QBLOCK)
            for h in range(2):
                pbuf[n, h, rows, :] = jnp.exp2(mm(qbuf[n, h, rows, :], kbuf[n, h], NT)).astype(BF)
    drain(rx.at[1], r_ax.at[1])
    for n in range(2):
        mat = matrix(n, 2)
        for i in range(span // 128):
            rows = slice(i * 128, (i + 1) * 128)
            act = active(rows, mat)
            for h in range(2):
                vext[n, h, rows, 0:HD] = act[:, h * HD : (h + 1) * HD].astype(BF)
        for b in range(span // QBLOCK):
            rows = slice(b * QBLOCK, (b + 1) * QBLOCK)
            for h in range(2):
                both = mm(pbuf[n, h, rows, :], vext[n, h])
                obuf[n, rows, h * HD : (h + 1) * HD] = (both[:, :HD] / both[:, HD:]).astype(BF)
        field = packed(obuf[n], matrix(n, 3))
        total = total + field if n else total - field

    tsend[...] = (total * lw_ref[0]).astype(BF)
    blocks = chips // 2
    trows = half // blocks

    def block_of(peer):
        return pl.ds(pl.multiple_of((peer["seq"] // 4 * L + peer["level"]) * trows, trows), trows)

    mine_b = block_of({"level": l, "seq": s})
    owner = core == z // L
    spot_b = 2 * (s // 2 * L + l) + core
    for step in steps(range(Z)):
        peer = on_chip(step, None)
        remote(tsend.at[block_of(peer)], b1.at[spot_b], s_b1, r_b1, peer)

    @pl.when(owner)
    def _():
        b1[spot_b] = tsend[mine_b, :]
        drain(b1.at[pl.ds(0, 2 * chips - 1)], r_b1)
        acc = b1[0].astype(F32)
        for i in range(1, 2 * chips):
            acc = acc + b1[i].astype(F32)
        gfull[mine_b, :] = acc.astype(BF)
        for peer in [on_chip(step, c) for step in steps((0, 1, 2, Z - 1)) for c in range(2)] + [{"seq": mate}]:
            remote(gfull.at[mine_b], gfull.at[mine_b], s_b3, r_b3, peer)
        drain(b1.at[pl.ds(0, blocks - 1)], r_b3)

    @pl.when(jnp.logical_not(owner))
    def _():
        remote(tsend.at[mine_b], b1.at[spot_b], s_b1, r_b1, {"seq": mate})
        drain(b1.at[pl.ds(0, blocks)], r_b3)

    cut = D // X
    side = cut // 2
    lane = lax.broadcasted_iota(jnp.int32, (half, 2 * chans), 1)
    scaling = jnp.where(lane < chans, rms[0:half, :], rms[half:, :])
    turned = (gfull[...].astype(F32) * scaling).T.astype(BF)
    for o in ((2, 1, 3) if X == 4 else tuple(range(1, X))) + (0,):
        to = lax.rem(d + o, X)
        cols = pl.ds(pl.multiple_of(to * cut + core * side, 128), side)
        term = mm(turned[:chans], fbuf[0:half, cols]) + mm(turned[chans:], fbuf[half:, cols])
        if o:
            psend[o - 1] = term.astype(BF)
            remote(psend.at[o - 1], crecv.at[d], s_c, r_c, {"dp": to})
        else:
            crecv[d] = term.astype(BF)

    rows_h = span // S
    first = s * rows_h
    which = first // half
    own = pl.ds(pl.multiple_of(first, rows_h), rows_h)
    g_own = gfull[pl.ds(pl.multiple_of(first - which * half, rows_h), rows_h), :].astype(F32)
    g_own = jnp.where(which == 0, g_own, pltpu.roll(g_own, chans, 1))[:, :chans]
    inner = jnp.sum(g_own * x0[own, :], axis=-1, keepdims=True) * (1.0 / D)
    scale_own = rms[own, 0:1]
    lessen = scale_own * inner
    g_own = g_own.astype(BF)
    for c in range(FEAT_CHUNKS):
        cols = slice(c * fc, (c + 1) * fc)
        grad = mm(g_own, gw[:, cols]) * gain[:, cols] - fbuf[own, cols].astype(F32) * lessen
        oh_ref[:, cols] = (grad * scale_own).astype(BF)

    drain(crecv.at[pl.ds(0, X - 1)], r_c)
    acc = crecv[0].astype(F32)
    for i in range(1, X):
        acc = acc + crecv[i].astype(F32)
    factor = 1.0 / math.sqrt(X * span)
    mine = pl.ds(pl.multiple_of(d * cut + core * side, 128), side)
    spot = pl.ds(pl.multiple_of(core * side, 128), side)
    ow_ref[:, spot] = acc * (gain[:, mine] * factor)
    remote(ow_ref.at[:, spot], ow_ref.at[:, spot], s_k, r_k, {"seq": mate})
    drain(psend, s_c)
    for n in range(2):
        drain(rx.at[n], s_rx.at[n])
        drain(rx.at[n], s_ax.at[n])
    drain(b1.at[pl.ds(0, chips - 1)], s_b1)

    @pl.when(owner)
    def _():
        drain(b1.at[pl.ds(0, 2 * blocks - 1)], s_b3)

    @pl.when(jnp.logical_not(owner))
    def _():
        drain(b1.at[0], s_b1)


    drain(ow_ref.at[:, 0:side], r_k)
    block = pl.ds(pl.multiple_of(d * cut, 128), cut)
    inside = jnp.sum(ow_ref[...] * gw[:, block].astype(F32), axis=0, keepdims=True)
    og_ref[...] = (inside / gain[:, block])[0]
    drain(ow_ref.at[:, 0:side], s_k)


def on_device(feats, gen_gain, gen_weight, noise, sigmas, level_weights, embed, proj_in, proj_out, head_out, qk_gain):
    sizes = L, S, X = tuple(lax.axis_size(a) for a in ("level", "seq", "dp"))
    span, D = feats.shape[1:]
    chans = gen_weight.shape[1]
    part = proj_in.shape[2]
    win_a = part if part % 128 == 0 else part + 64
    win_s = D // S if D // S % 128 == 0 else D // S + 64
    half = span // 2
    side = D // X // 2
    rows_h = span // S
    hbm = pl.BlockSpec(memory_space=pltpu.HBM)
    vmem = pl.BlockSpec(memory_space=pltpu.VMEM)
    smem = pl.BlockSpec(memory_space=pltpu.SMEM)
    V = pltpu.VMEM
    dma = pltpu.SemaphoreType.DMA
    scratch = [
        V((4, HD), F32),
        V((span, D), BF), V((1, D), F32), V((chans, D), BF), V((chans, span), F32),
        V((2, chans, win_a), BF), V((2, chans, win_a), BF), V((2, chans, win_s), BF), V((2, chans, win_s), BF),
        V((2, 4, win_a, 2 * HD), BF),
        V((2, 8 * chans, HD), BF), V((2, L * X - 1, 8 * chans // (L * X), HD), BF), V((2, 8 * chans, HD), BF),
        V((span, 128), F32), V((span, chans), F32), V((span, 128), F32), V((span, chans), BF),
        V((2, 2, span, HD), BF), V((2, 2, span, HD), BF), V((2, 2, span, span), BF),
        V((2, 2, span, 2 * HD), BF), V((2, span, 2 * HD), BF),
        V((half, 2 * chans), BF), V((L * S, 4 * half // (L * S), 2 * chans), BF),
        V((half, 2 * chans), BF), V((X - 1, chans, side), BF), V((X, chans, side), BF),
        dma((12,)), dma((FEAT_CHUNKS,)),
    ] + [dma((2,))] * 4 + [dma] * 8
    out_h, out_w, out_g = pl.pallas_call(
        functools.partial(kernel, sizes),
        out_shape=(
            V((rows_h, D), BF),
            V((chans, 2 * side), F32),
            V((2 * side,), F32),
        ),
        in_specs=[smem] * 2 + [hbm] * 9,
        out_specs=(vmem, vmem, vmem),
        scratch_shapes=scratch,
        compiler_params=pltpu.CompilerParams(
            collective_id=0, has_side_effects=True, vmem_limit_bytes=40 * 1024 * 1024
        ),
    )(
        sigmas,
        level_weights,
        *(
            pltpu.with_memory_space_constraint(a, pltpu.HBM)
            for a in (
                qk_gain.reshape(4, HD), feats, gen_gain[None], gen_weight.T, noise[0, 0].T,
                embed, proj_in, jnp.swapaxes(proj_out, 1, 2), jnp.swapaxes(head_out, 1, 2),
            )
        ),
    )
    return out_h[None], out_w.T, out_g


def solution(mesh):
    in_specs = (
        P("dp", None, None),
        P(),
        P(),
        P("level", "dp", None, None),
        P("level"),
        P("level"),
        P(),
        P(None, None, ("level", "dp"), "seq"),
        P(None, "seq", ("level", "dp")),
        P(),
        P(),
    )
    out_specs = (P("dp", "seq", None), P("dp", None), P("dp"))
    return jax.shard_map(on_device, mesh=mesh, in_specs=in_specs, out_specs=out_specs, check_vma=False)
```
